256 devices in a mesh: tm: 16 (over z, y_hi), az: 2 (over y_lo), rg: 8 (over x, core).
Axes of the slice: x: 4, y: 4 (y_hi: 2, y_lo: 2; y = y_hi * 2 + y_lo), z: 8, core: 2. Of those that a mesh axis runs over, the one named last changes fastest.
Arguments:
- slc: bfloat16 [16, 2, 128, 4096], P('tm', None, 'az', 'rg')
- pairs: int32 [16, 3], P('tm'), may hold values from 0 to 15, as said below
Outputs:
- filtered: float32 [16, 3, 2, 32, 256], P('tm', None, None, 'az', 'rg')
- coherence: float32 [16, 3, 32, 256], P('tm', None, 'az', 'rg')
The draws below stay inside these ranges and needn't reach their ends.
Inputs may be any that keep to these rules, and one draw needn't show every extreme that they name: `pairs`: row a holds 3 different acquisitions, each between 1 and 3 away from a.
All inputs are finite; a program needn't handle non-finite values.
Results may differ from the reference program's by a relative error of at most 0.0003.
Values may be sent and summed in bfloat16 or wider, within the bound.
No kernel may reach another device: no remote copies, remote signals or barrier semaphores. Data moves between devices by JAX's collectives and lax.ppermute only.
A program may use at most 128 MiB of HBM per device.

```python
import math
import jax
import jax.numpy as jnp
from jax import lax

NACQ = 16
NAZ = 128
NRG = 4096


def draw_slc(key, part):
    key = jax.random.fold_in(key, 11)
    keys = jax.random.split(key, 5)
    sigma = jnp.exp(jax.random.uniform(keys[0], (NACQ,), jnp.float32, math.log(0.3), math.log(2.0)))
    rate_az = jax.random.uniform(keys[1], (NACQ,), jnp.float32, -1.0, 1.0)
    rate_rg = jax.random.uniform(keys[2], (NACQ,), jnp.float32, -1.0, 1.0)
    scene = jax.random.normal(keys[3], (2, NAZ, NRG), jnp.float32)
    noise = jax.random.normal(keys[4], (NACQ, 2, NAZ, NRG), jnp.float32)
    lines = jnp.arange(NAZ, dtype=jnp.float32)[:, None]
    columns = jnp.arange(NRG, dtype=jnp.float32)[None, :]
    phase = 2.0 * math.pi * (rate_az[:, None, None] * lines / 160.0 + rate_rg[:, None, None] * columns / 640.0)
    cosine = jnp.cos(phase)
    sine = jnp.sin(phase)
    rot_real = scene[0] * cosine - scene[1] * sine
    rot_imag = scene[0] * sine + scene[1] * cosine
    mixed = jnp.stack([rot_real, rot_imag], axis=1) + sigma[:, None, None, None] * noise
    mixed = mixed / jnp.sqrt(1.0 + sigma * sigma)[:, None, None, None]
    return mixed.astype(jnp.bfloat16)


def draw_pairs(key, part):
    key = jax.random.fold_in(key, 5)
    offsets = jnp.array([-3, -2, -1, 1, 2, 3], jnp.int32)
    rows = jnp.arange(NACQ, dtype=jnp.int32)[:, None]
    target = rows + offsets[None, :]
    valid = (target >= 0) & (target < NACQ)
    score = jax.random.randint(key, (NACQ, 6), 0, 1 << 20, jnp.int32) * 8 + jnp.arange(6, dtype=jnp.int32)[None, :]
    slots = jnp.arange(6, dtype=jnp.int32)[None, :]
    forced = (rows == 1) & (slots == 2) | (rows == NACQ - 2) & (slots == 3)
    score = jnp.where(forced, (1 << 24) + slots, score)
    score = jnp.where(valid, score, -1)
    chosen_score, picked = lax.top_k(score, 3)
    return jnp.take_along_axis(target, picked, axis=1).astype(jnp.int32)


def setup_inputs(seed: int = 0) -> dict:
    key_list = jax.random.split(jax.random.key(seed), 3)
    return {
        "slc": draw_slc(jax.random.fold_in(key_list[2], 71), 0),
        "pairs": draw_pairs(jax.random.fold_in(key_list[2], 71), 0),
    }


def multilook(values):
    lines = values.shape[-2]
    columns = values.shape[-1]
    shaped = values.reshape(values.shape[:-2] + (lines // 4, 4, columns // 16, 16))
    return lax.optimization_barrier(jnp.sum(shaped, axis=(-3, -1))) / 64.0

def pair_fields(own_tile, remote_tiles):
    own_real = own_tile[0]
    own_imag = own_tile[1]
    far_real = remote_tiles[:, 0]
    far_imag = remote_tiles[:, 1]
    cross_real = multilook(own_real * far_real + own_imag * far_imag)
    cross_imag = multilook(own_imag * far_real - own_real * far_imag)
    far_power = multilook(far_real * far_real + far_imag * far_imag)
    own_power = multilook(own_real * own_real + own_imag * own_imag)[None]
    return jnp.concatenate([cross_real, cross_imag, far_power, own_power], axis=0)

def cut_patches(values):
    lines = values.shape[-2]
    columns = values.shape[-1]
    leading = values.shape[:-2]
    blocks = values.reshape(leading + (lines // 16, 16, columns // 16, 16))
    by_rows = jnp.concatenate([blocks[..., :-1, :, :, :], blocks[..., 1:, :, :, :]], axis=-3)
    return jnp.concatenate([by_rows[..., :-1, :], by_rows[..., 1:, :]], axis=-1)

def add_patches(patches):
    by_rows = patches[..., :-1, 16:, :, :] + patches[..., 1:, :16, :, :]
    joined = by_rows[..., :-1, 16:] + by_rows[..., 1:, :16]
    shape = joined.shape
    return joined.reshape(shape[:-4] + (shape[-4] * 16, shape[-2] * 16))

def taper_weights():
    steps = jnp.arange(32, dtype=jnp.float32)
    single = jnp.sin(math.pi * (steps + 0.5) / 32.0) ** 2
    return single[:, None, None] * single

def smooth_response(spectral_amplitude):
    smoothed = jnp.zeros_like(spectral_amplitude)
    for shift_a in (-1, 0, 1):
        for shift_b in (-1, 0, 1):
            smoothed = smoothed + jnp.roll(spectral_amplitude, (shift_a, shift_b), axis=(-3, -1))
    response = jnp.sqrt(smoothed / 9.0)
    largest = lax.optimization_barrier(jnp.max(response, axis=(-3, -1), keepdims=True))
    return response / (largest + 1e-06)

def goldstein(field_real, field_imag):
    power_spectrum = jnp.fft.fftn(cut_patches(field_real) + 1j * cut_patches(field_imag), axes=(-3, -1))
    weights = smooth_response(jnp.abs(power_spectrum))
    restored = jnp.fft.ifftn(power_spectrum * weights, axes=(-3, -1))
    taper_window = taper_weights()
    return (add_patches(restored.real * taper_window), add_patches(restored.imag * taper_window))

def window_sum(values, lines, columns):
    total = jnp.zeros(values.shape[:-2] + (lines, columns), values.dtype)
    for shift_a in range(5):
        for shift_b in range(5):
            total = total + values[..., shift_a:shift_a + lines, shift_b:shift_b + columns]
    return total

def coherence_of(fields):
    lines = fields.shape[-2] - 32
    columns = fields.shape[-1] - 32
    inner = fields[:, 14:18 + lines, 14:18 + columns]
    real_total_sum = window_sum(inner[0:3], lines, columns)
    sum_imag = window_sum(inner[3:6], lines, columns)
    far_sum = window_sum(inner[6:9], lines, columns)
    own_sum = window_sum(inner[9:10], lines, columns)
    return jnp.sqrt(real_total_sum * real_total_sum + sum_imag * sum_imag) / jnp.sqrt(own_sum * far_sum)

def reference(slc, pairs):
    samples = slc.astype(jnp.float32)

    def acq_fields(acq_index):
        own_tile = samples[acq_index]
        remote_tiles = jnp.take(samples, pairs[acq_index], axis=0)
        return pair_fields(own_tile, remote_tiles)
    fields = lax.map(acq_fields, jnp.arange(NACQ, dtype=jnp.int32))
    padded = jnp.pad(fields, ((0, 0), (0, 0), (16, 16), (16, 16)))

    def finish(block):
        filt_real, filt_imag = goldstein(block[0:3], block[3:6])
        return (jnp.stack([filt_real, filt_imag], axis=1), coherence_of(block))
    filtered, coherence = lax.map(finish, padded)
    return (filtered, coherence)
```

```python
import math

import jax
import jax.numpy as jnp
import ml_dtypes
import numpy as np
from jax import lax
from jax.experimental import pallas as pl
from jax.experimental.pallas import tpu as pltpu
from jax.sharding import Mesh, PartitionSpec as P

F32 = jnp.float32
BF16 = jnp.bfloat16
EVERY = ("tm", "az", "rg")


def split_table(table):
    high = table.astype(ml_dtypes.bfloat16)
    low = (table - high.astype(np.float64)).astype(ml_dtypes.bfloat16)
    return high, low


def column_tables():
    forward = np.zeros((256, 384))
    back = np.zeros((256, 256))
    steps = np.arange(32)
    taper = np.sin(math.pi * (steps + 0.5) / 32.0) ** 2

    def row_of(field, column):
        if column < 16:
            return 128 + field * 32 + 16 + column
        if column < 48:
            return field * 32 + column - 16
        return 128 + field * 32 + column - 48

    for patch in range(3):
        for j in range(32):
            angle = 2.0 * math.pi * (j * steps % 32) / 32.0
            real, imag = row_of(0, patch * 16 + j), row_of(1, patch * 16 + j)
            at = patch * 32 + steps
            forward[real, at] = np.cos(angle)
            forward[imag, at] = np.sin(angle)
            forward[real, 128 + at] = -np.sin(angle)
            forward[imag, 128 + at] = np.cos(angle)
            column = patch * 16 + j - 16
            if 0 <= column < 32:
                scale = taper[j] / 32.0
                back[at, column] = np.cos(angle) * scale
                back[128 + at, column] = -np.sin(angle) * scale
                back[at, 128 + column] = np.sin(angle) * scale
                back[128 + at, 128 + column] = np.cos(angle) * scale
    for field in range(4):
        for cell in range(32):
            for column in range(cell + 14, cell + 19):
                forward[row_of(field, column), 256 + field * 32 + cell] = 1.0
    return forward, back


def line_tables():
    forward = np.zeros((2, 128, 64))
    window = np.zeros((2, 16, 32))
    back = np.zeros((32, 128))
    steps = np.arange(32)
    taper = np.sin(math.pi * (steps + 0.5) / 32.0) ** 2
    for side in range(2):
        places = {}
        for line in range(16):
            places[16 + line] = line
            places[(32 if side == 0 else 0) + line] = 16 + line
        for patch in range(2):
            for j in range(32):
                row = places.get(patch * 16 + j)
                if row is None:
                    continue
                angle = 2.0 * math.pi * (j * steps % 32) / 32.0
                at = patch * 32 + steps
                forward[side, at, row] = np.cos(angle)
                forward[side, at, 32 + row] = np.sin(angle)
                forward[side, 64 + at, row] = -np.sin(angle)
                forward[side, 64 + at, 32 + row] = np.cos(angle)
        for cell in range(16):
            for line in range(cell + 14, cell + 19):
                if line in places:
                    window[side, cell, places[line]] = 1.0
    for patch in range(2):
        for j in range(32):
            cell = patch * 16 + j - 16
            if 0 <= cell < 16:
                angle = 2.0 * math.pi * (j * steps % 32) / 32.0
                scale = taper[j] / 32.0
                at = patch * 32 + steps
                back[cell, at] = np.cos(angle) * scale
                back[cell, 64 + at] = -np.sin(angle) * scale
                back[16 + cell, at] = np.sin(angle) * scale
                back[16 + cell, 64 + at] = np.cos(angle) * scale
    return forward, window, back


def tables():
    column_forward, column_back = column_tables()
    line_forward, window, line_back = line_tables()
    cf_high, cf_low = split_table(column_forward)
    cb_high, cb_low = split_table(column_back)
    lf_high, lf_low = split_table(line_forward)
    lb_high, lb_low = split_table(line_back)
    return (
        cf_high,
        cf_low,
        np.concatenate([lf_high, lf_high, lf_low], axis=2),
        np.concatenate([window, window], axis=2).astype(ml_dtypes.bfloat16),
        np.concatenate([lb_high, lb_high, lb_low], axis=1),
        cb_high,
        cb_low,
    )


def look_table():
    table = np.zeros((512, 128))
    columns = np.arange(512)
    table[columns, columns // 16] = 1.0 / 64.0
    return table.astype(ml_dtypes.bfloat16)


def halves(values):
    high = values.astype(BF16)
    low = (values - high.astype(F32)).astype(BF16)
    return high, low


def dot(left, right):
    return jnp.dot(left, right, preferred_element_type=F32)


def cross_kernel(own, other, up, down, far, look, own_out, other_out, wide, sums):
    tiles = (own, other, up, down, far)
    for index, tile in enumerate(tiles):
        for part in range(2):
            for chunk in range(4):
                wide[index * 2 + part, chunk] = tile[part, :, chunk * 128 : chunk * 128 + 128].astype(F32)
    couples = ((0, 1), (0, 2), (0, 3), (1, 2), (1, 3), (1, 4))
    for chunk in range(4):
        at = slice(chunk * 128, chunk * 128 + 128)
        totals = [None] * 17
        for line in range(4):
            real = [wide[2 * i, chunk, pl.ds(line, 16, stride=4), :] for i in range(5)]
            imag = [wide[2 * i + 1, chunk, pl.ds(line, 16, stride=4), :] for i in range(5)]
            terms = []
            for u, v in couples:
                terms.append(real[u] * real[v] + imag[u] * imag[v])
            for u, v in couples:
                terms.append(imag[u] * real[v] - real[u] * imag[v])
            for u in range(5):
                terms.append(real[u] * real[u] + imag[u] * imag[u])
            totals = [t if s is None else s + t for s, t in zip(totals, terms)]
        for index, total in enumerate(totals):
            sums[index * 16 : index * 16 + 16, at] = total
    high, low = halves(sums[...])
    table = look[...]
    looked = dot(high, table) + dot(low, table)
    fields = [looked[i * 16 : i * 16 + 16] for i in range(17)]
    far_power = [pltpu.roll(fields[12 + i], 64, 1) for i in range(5)]
    own_power = [pltpu.roll(fields[12 + i], 96, 1) for i in range(2)]
    for index, (u, v) in enumerate(couples):
        row = fields[index] + pltpu.roll(fields[6 + index], 32, 1) + far_power[v] + own_power[u]
        if u == 0:
            own_out[index] = row
        else:
            other_out[index - 3] = row


def choose_kernel(meta, own, swapped, own_beside, swapped_beside, out):
    position = meta[0]
    odd = position % 2
    for slot in range(3):
        offset = meta[4 + slot] - position
        flipped = jnp.where(odd == 1, -offset, offset)
        near = jnp.where(flipped == 1, 0, jnp.where(offset == 2, 1, 2))
        third = jnp.where(odd == 1, 4, 3)
        first = jnp.where(odd == 1, 3, 4)
        away = jnp.where(flipped == 3, third, jnp.where(flipped == -1, first, 5)) - 3
        is_near = (flipped == 1) | (offset == 2) | (offset == -2)
        near = jnp.where(is_near, near, 0)
        away = jnp.where(is_near, 0, away)
        out[slot, 0:16] = jnp.where(is_near, own[near], swapped[away])
        out[slot, 16:32] = jnp.where(is_near, own_beside[near], swapped_beside[away])


def finish_kernel(
    meta, fields, core_halo, chip_halo, cf_high, cf_low, lf, window, lb, cb_high, cb_low, filtered, coherence
):
    side = meta[1]
    core = meta[2]
    lane = lax.broadcasted_iota(jnp.int32, (1, 128), 1)
    place = lane % 32
    from_core = (place >= 16) == (core == 1)
    halo = jnp.where(from_core, core_halo[...].reshape(96, 128), chip_halo[...].reshape(96, 128))
    values = jnp.concatenate([fields[...].reshape(96, 128), halo], axis=1)
    high, low = halves(values)
    table = cf_high[...]
    mixed = dot(high, table) + dot(low, table) + dot(high, cf_low[...])
    rows = [mixed[32 * s : 32 * s + 32] for s in range(3)]
    real = jnp.concatenate([r[:, 0:128] for r in rows], axis=1)
    imag = jnp.concatenate([r[:, 128:256] for r in rows], axis=1)
    sums = jnp.concatenate([r[:, 256:384] for r in rows], axis=1)
    high, low = halves(jnp.concatenate([real, imag], axis=0))
    spectrum = dot(lf[side], jnp.concatenate([high, low, high], axis=0))
    spec_real, spec_imag = spectrum[0:64], spectrum[64:128]
    power = jnp.sqrt(spec_real * spec_real + spec_imag * spec_imag)

    def turned(block, by):
        away = pltpu.roll(block, by % 128, 1)
        wrapped = pltpu.roll(block, (by - 32) % 128, 1)
        if by > 0:
            return jnp.where(place < by, wrapped, away)
        wrapped = pltpu.roll(block, (by + 32) % 128, 1)
        return jnp.where(place >= 32 + by, wrapped, away)

    smoothed = []
    for patch in range(2):
        for slot in range(3):
            block = power[32 * patch : 32 * patch + 32, 128 * slot : 128 * slot + 128]
            block = block + pltpu.roll(block, 1, 0) + pltpu.roll(block, 31, 0)
            block = block + turned(block, 1) + turned(block, -1)
            smoothed.append(block / 9.0)
    largest = jnp.concatenate([jnp.max(b, axis=0, keepdims=True) for b in smoothed] + [jnp.zeros((2, 128), F32)], axis=0)
    for by in (1, 2, 4, 8, 16):
        largest = jnp.maximum(largest, turned(largest, by))
    scale = 1.0 / (jnp.sqrt(largest) + 1e-06)
    weights = [jnp.sqrt(b) * scale[i : i + 1] for i, b in enumerate(smoothed)]
    weights = jnp.concatenate(
        [jnp.concatenate(weights[0:3], axis=1), jnp.concatenate(weights[3:6], axis=1)], axis=0
    )
    high, low = halves(jnp.concatenate([spec_real * weights, spec_imag * weights], axis=0))
    lines = dot(lb[...], jnp.concatenate([high, low, high], axis=0))
    stacked = jnp.concatenate(
        [
            jnp.concatenate([lines[0:16, 128 * s : 128 * s + 128], lines[16:32, 128 * s : 128 * s + 128]], axis=1)
            for s in range(3)
        ],
        axis=0,
    )
    high, low = halves(stacked)
    table = cb_high[...]
    result = dot(high, table) + dot(low, table) + dot(high, cb_low[...])
    for slot in range(3):
        filtered[slot, 0] = result[16 * slot : 16 * slot + 16, 0:32]
        filtered[slot, 1] = result[16 * slot : 16 * slot + 16, 128:160]

    high, low = halves(sums)
    totals = dot(window[side], jnp.concatenate([high, low], axis=0))
    for slot in range(3):
        total = totals[:, 128 * slot : 128 * slot + 128]
        square = total * total
        square = square + pltpu.roll(square, 96, 1)
        product = total * pltpu.roll(total, 96, 1)
        product = pltpu.roll(product, 64, 1)
        coherence[slot] = (jnp.sqrt(square) / jnp.sqrt(product))[:, 0:32]


VMEM = pl.BlockSpec(memory_space=pltpu.VMEM)
SMEM = pl.BlockSpec(memory_space=pltpu.SMEM)


def moved(value, where):
    pairs = []
    for z in range(8):
        for yh in range(2):
            for yl in range(2):
                for r in range(8):
                    target = where(z, yh, yl, r)
                    if target is None:
                        continue
                    tz, th, tl, tr = target
                    if not (0 <= tz < 8 and 0 <= tr < 8):
                        continue
                    pairs.append((((z * 2 + yh) * 2 + yl) * 8 + r, ((tz * 2 + th) * 2 + tl) * 8 + tr))
    return lax.ppermute(value, EVERY, pairs)


def per_device(slc, pairs):
    tile = slc[0]
    position = lax.axis_index("tm")
    side = lax.axis_index("az")
    column = lax.axis_index("rg")
    meta = jnp.stack([position, side, column % 2, 0, pairs[0, 0], pairs[0, 1], pairs[0, 2], 0]).astype(jnp.int32)

    def even_pair(z, h, l, r):
        return (z ^ 1, h, l, r)

    def odd_pair(z, h, l, r):
        return (((z + 1) ^ 1) - 1, h, l, r)

    def far_pair(z, h, l, r):
        return (z - 2, h, l, r) if h == 0 else (z + 2, h, l, r)

    swap_even = moved(tile, even_pair)
    swap_odd = moved(tile, odd_pair)
    far = moved(tile, far_pair)
    other = moved(tile, lambda z, h, l, r: (z, 1 - h, l, r))
    odd_z = (position // 2) % 2 == 1
    up = jnp.where(odd_z, swap_odd, swap_even)
    down = jnp.where(odd_z, swap_even, swap_odd)

    record = jax.ShapeDtypeStruct((3, 16, 128), F32)
    own_fields, other_fields = pl.pallas_call(
        cross_kernel,
        out_shape=(record, record),
        in_specs=[VMEM] * 6,
        out_specs=(VMEM, VMEM),
        scratch_shapes=[pltpu.VMEM((10, 4, 64, 128), F32), pltpu.VMEM((272, 512), F32)],
        compiler_params=pltpu.CompilerParams(vmem_limit_bytes=24 * 2**20),
        name="cross",
    )(tile, other, up, down, far, jnp.asarray(look_table()))

    swapped = moved(other_fields, lambda z, h, l, r: (z, 1 - h, l, r))
    own_beside = moved(own_fields, lambda z, h, l, r: (z, h, 1 - l, r))
    swapped_beside = moved(other_fields, lambda z, h, l, r: (z, 1 - h, 1 - l, r))
    fields = pl.pallas_call(
        choose_kernel,
        out_shape=jax.ShapeDtypeStruct((3, 32, 128), F32),
        in_specs=[SMEM] + [VMEM] * 4,
        out_specs=VMEM,
        name="choose",
    )(meta, own_fields, swapped, own_beside, swapped_beside)

    core_halo = moved(fields, lambda z, h, l, r: (z, h, l, r ^ 1))
    chip_halo = moved(fields, lambda z, h, l, r: (z, h, l, ((r + 1) ^ 1) - 1))
    filtered, coherence = pl.pallas_call(
        finish_kernel,
        out_shape=(jax.ShapeDtypeStruct((3, 2, 16, 32), F32), jax.ShapeDtypeStruct((3, 16, 32), F32)),
        in_specs=[SMEM] + [VMEM] * 10,
        out_specs=(VMEM, VMEM),
        compiler_params=pltpu.CompilerParams(vmem_limit_bytes=24 * 2**20),
        name="finish",
    )(meta, fields, core_halo, chip_halo, *[jnp.asarray(t) for t in tables()])
    return (filtered[None], coherence[None])


def solution(mesh):
    placed = (P("tm", None, "az", "rg"), P("tm", None))
    return jax.shard_map(
        per_device,
        mesh=mesh,
        in_specs=placed,
        out_specs=(P("tm", None, None, "az", "rg"), P("tm", None, "az", "rg")),
        check_vma=False,
    )
```

```python
import math

import jax
import jax.numpy as jnp
import ml_dtypes
import numpy as np
from jax import lax
from jax.experimental import pallas as pl
from jax.experimental.pallas import tpu as pltpu
from jax.sharding import Mesh, PartitionSpec as P

F32 = jnp.float32
BF16 = jnp.bfloat16
EVERY = ("tm", "az", "rg")


def split_table(table):
    high = table.astype(ml_dtypes.bfloat16)
    low = (table - high.astype(np.float64)).astype(ml_dtypes.bfloat16)
    return high, low


def column_tables():
    forward = np.zeros((256, 384))
    back = np.zeros((256, 256))
    steps = np.arange(32)
    taper = np.sin(math.pi * (steps + 0.5) / 32.0) ** 2

    def row_of(field, column):
        if column < 16:
            return 128 + field * 32 + 16 + column
        if column < 48:
            return field * 32 + column - 16
        return 128 + field * 32 + column - 48

    for patch in range(3):
        for j in range(32):
            angle = 2.0 * math.pi * (j * steps % 32) / 32.0
            real, imag = row_of(0, patch * 16 + j), row_of(1, patch * 16 + j)
            at = patch * 32 + steps
            forward[real, at] = np.cos(angle)
            forward[imag, at] = np.sin(angle)
            forward[real, 128 + at] = -np.sin(angle)
            forward[imag, 128 + at] = np.cos(angle)
            column = patch * 16 + j - 16
            if 0 <= column < 32:
                scale = taper[j] / 32.0
                back[at, column] = np.cos(angle) * scale
                back[128 + at, column] = -np.sin(angle) * scale
                back[at, 128 + column] = np.sin(angle) * scale
                back[128 + at, 128 + column] = np.cos(angle) * scale
    for field in range(4):
        for cell in range(32):
            for column in range(cell + 14, cell + 19):
                forward[row_of(field, column), 256 + field * 32 + cell] = 1.0
    return forward, back


def line_tables():
    forward = np.zeros((2, 128, 64))
    window = np.zeros((2, 16, 32))
    back = np.zeros((32, 128))
    steps = np.arange(32)
    taper = np.sin(math.pi * (steps + 0.5) / 32.0) ** 2
    for side in range(2):
        places = {}
        for line in range(16):
            places[16 + line] = line
            places[(32 if side == 0 else 0) + line] = 16 + line
        for patch in range(2):
            for j in range(32):
                row = places.get(patch * 16 + j)
                if row is None:
                    continue
                angle = 2.0 * math.pi * (j * steps % 32) / 32.0
                at = patch * 32 + steps
                forward[side, at, row] = np.cos(angle)
                forward[side, at, 32 + row] = np.sin(angle)
                forward[side, 64 + at, row] = -np.sin(angle)
                forward[side, 64 + at, 32 + row] = np.cos(angle)
        for cell in range(16):
            for line in range(cell + 14, cell + 19):
                if line in places:
                    window[side, cell, places[line]] = 1.0
    for patch in range(2):
        for j in range(32):
            cell = patch * 16 + j - 16
            if 0 <= cell < 16:
                angle = 2.0 * math.pi * (j * steps % 32) / 32.0
                scale = taper[j] / 32.0
                at = patch * 32 + steps
                back[cell, at] = np.cos(angle) * scale
                back[cell, 64 + at] = -np.sin(angle) * scale
                back[16 + cell, at] = np.sin(angle) * scale
                back[16 + cell, 64 + at] = np.cos(angle) * scale
    return forward, window, back


def tables():
    column_forward, column_back = column_tables()
    line_forward, window, line_back = line_tables()
    cf_high, cf_low = split_table(column_forward)
    cb_high, cb_low = split_table(column_back)
    lf_high, lf_low = split_table(line_forward)
    lb_high, lb_low = split_table(line_back)
    return (
        cf_high,
        cf_low,
        np.concatenate([lf_high, lf_high, lf_low], axis=2),
        np.concatenate([window, window], axis=2).astype(ml_dtypes.bfloat16),
        np.concatenate([lb_high, lb_high, lb_low], axis=1),
        cb_high,
        cb_low,
    )


def look_table():
    table = np.zeros((512, 128))
    columns = np.arange(512)
    table[columns, columns // 16] = 1.0 / 64.0
    return table.astype(ml_dtypes.bfloat16)


def halves(values):
    high = values.astype(BF16)
    low = (values - high.astype(F32)).astype(BF16)
    return high, low


def dot(left, right):
    return jnp.dot(left, right, preferred_element_type=F32)


def cross_kernel(own, other, up, down, far, look, own_out, other_out, wide, sums):
    tiles = (own, other, up, down, far)
    for index, tile in enumerate(tiles):
        for part in range(2):
            for chunk in range(4):
                wide[index * 2 + part, chunk] = tile[part, :, chunk * 128 : chunk * 128 + 128].astype(F32)
    couples = ((0, 1), (0, 2), (0, 3), (1, 2), (1, 3), (1, 4))
    for chunk in range(4):
        at = slice(chunk * 128, chunk * 128 + 128)
        totals = [None] * 17
        for line in range(4):
            real = [wide[2 * i, chunk, pl.ds(line, 16, stride=4), :] for i in range(5)]
            imag = [wide[2 * i + 1, chunk, pl.ds(line, 16, stride=4), :] for i in range(5)]
            terms = []
            for u, v in couples:
                terms.append(real[u] * real[v] + imag[u] * imag[v])
            for u, v in couples:
                terms.append(imag[u] * real[v] - real[u] * imag[v])
            for u in range(5):
                terms.append(real[u] * real[u] + imag[u] * imag[u])
            totals = [t if s is None else s + t for s, t in zip(totals, terms)]
        for index, total in enumerate(totals):
            sums[index * 16 : index * 16 + 16, at] = total
    high, low = halves(sums[...])
    table = look[...]
    looked = dot(high, table) + dot(low, table)
    fields = [looked[i * 16 : i * 16 + 16] for i in range(17)]
    far_power = [pltpu.roll(fields[12 + i], 64, 1) for i in range(5)]
    own_power = [pltpu.roll(fields[12 + i], 96, 1) for i in range(2)]
    for index, (u, v) in enumerate(couples):
        row = fields[index] + pltpu.roll(fields[6 + index], 32, 1) + far_power[v] + own_power[u]
        if u == 0:
            own_out[index] = row
        else:
            other_out[index - 3] = row


def choose_kernel(pairs, own, swapped, own_beside, swapped_beside, out):
    position = lax.axis_index("tm")
    odd = position % 2
    for slot in range(3):
        offset = pairs[0, slot] - position
        flipped = jnp.where(odd == 1, -offset, offset)
        near = jnp.where(flipped == 1, 0, jnp.where(offset == 2, 1, 2))
        third = jnp.where(odd == 1, 4, 3)
        first = jnp.where(odd == 1, 3, 4)
        away = jnp.where(flipped == 3, third, jnp.where(flipped == -1, first, 5)) - 3
        is_near = (flipped == 1) | (offset == 2) | (offset == -2)
        near = jnp.where(is_near, near, 0)
        away = jnp.where(is_near, 0, away)
        out[slot, 0:16] = jnp.where(is_near, own[near], swapped[away])
        out[slot, 16:32] = jnp.where(is_near, own_beside[near], swapped_beside[away])


def finish_kernel(
    fields, core_halo, chip_halo, cf_high, cf_low, lf, window, lb, cb_high, cb_low, filtered, coherence
):
    side = lax.axis_index("az")
    core = lax.axis_index("rg") % 2
    lane = lax.broadcasted_iota(jnp.int32, (1, 128), 1)
    place = lane % 32
    from_core = (place >= 16) == (core == 1)
    halo = jnp.where(from_core, core_halo[...].reshape(96, 128), chip_halo[...].reshape(96, 128))
    values = jnp.concatenate([fields[...].reshape(96, 128), halo], axis=1)
    high, low = halves(values)
    table = cf_high[...]
    mixed = dot(high, table) + dot(low, table) + dot(high, cf_low[...])
    rows = [mixed[32 * s : 32 * s + 32] for s in range(3)]
    real = jnp.concatenate([r[:, 0:128] for r in rows], axis=1)
    imag = jnp.concatenate([r[:, 128:256] for r in rows], axis=1)
    sums = jnp.concatenate([r[:, 256:384] for r in rows], axis=1)
    high, low = halves(jnp.concatenate([real, imag], axis=0))
    spectrum = dot(lf[side], jnp.concatenate([high, low, high], axis=0))
    spec_real, spec_imag = spectrum[0:64], spectrum[64:128]
    power = jnp.sqrt(spec_real * spec_real + spec_imag * spec_imag)

    def turned(block, by):
        away = pltpu.roll(block, by % 128, 1)
        wrapped = pltpu.roll(block, (by - 32) % 128, 1)
        if by > 0:
            return jnp.where(place < by, wrapped, away)
        wrapped = pltpu.roll(block, (by + 32) % 128, 1)
        return jnp.where(place >= 32 + by, wrapped, away)

    smoothed = []
    for patch in range(2):
        for slot in range(3):
            block = power[32 * patch : 32 * patch + 32, 128 * slot : 128 * slot + 128]
            block = block + pltpu.roll(block, 1, 0) + pltpu.roll(block, 31, 0)
            block = block + turned(block, 1) + turned(block, -1)
            smoothed.append(block / 9.0)
    largest = jnp.concatenate([jnp.max(b, axis=0, keepdims=True) for b in smoothed] + [jnp.zeros((2, 128), F32)], axis=0)
    for by in (1, 2, 4, 8, 16):
        largest = jnp.maximum(largest, turned(largest, by))
    scale = 1.0 / (jnp.sqrt(largest) + 1e-06)
    weights = [jnp.sqrt(b) * scale[i : i + 1] for i, b in enumerate(smoothed)]
    weights = jnp.concatenate(
        [jnp.concatenate(weights[0:3], axis=1), jnp.concatenate(weights[3:6], axis=1)], axis=0
    )
    high, low = halves(jnp.concatenate([spec_real * weights, spec_imag * weights], axis=0))
    lines = dot(lb[...], jnp.concatenate([high, low, high], axis=0))
    stacked = jnp.concatenate(
        [
            jnp.concatenate([lines[0:16, 128 * s : 128 * s + 128], lines[16:32, 128 * s : 128 * s + 128]], axis=1)
            for s in range(3)
        ],
        axis=0,
    )
    high, low = halves(stacked)
    table = cb_high[...]
    result = dot(high, table) + dot(low, table) + dot(high, cb_low[...])
    for slot in range(3):
        filtered[slot, 0] = result[16 * slot : 16 * slot + 16, 0:32]
        filtered[slot, 1] = result[16 * slot : 16 * slot + 16, 128:160]

    high, low = halves(sums)
    totals = dot(window[side], jnp.concatenate([high, low], axis=0))
    for slot in range(3):
        total = totals[:, 128 * slot : 128 * slot + 128]
        square = total * total
        square = square + pltpu.roll(square, 96, 1)
        product = total * pltpu.roll(total, 96, 1)
        product = pltpu.roll(product, 64, 1)
        coherence[slot] = (jnp.sqrt(square) / jnp.sqrt(product))[:, 0:32]


VMEM = pl.BlockSpec(memory_space=pltpu.VMEM)
SMEM = pl.BlockSpec(memory_space=pltpu.SMEM)


def moved(value, where):
    pairs = []
    for z in range(8):
        for yh in range(2):
            for yl in range(2):
                for r in range(8):
                    target = where(z, yh, yl, r)
                    if target is None:
                        continue
                    tz, th, tl, tr = target
                    if not (0 <= tz < 8 and 0 <= tr < 8):
                        continue
                    pairs.append((((z * 2 + yh) * 2 + yl) * 8 + r, ((tz * 2 + th) * 2 + tl) * 8 + tr))
    return lax.ppermute(value, EVERY, pairs)


def per_device(slc, pairs):
    tile = slc[0]
    position = lax.axis_index("tm")

    def even_pair(z, h, l, r):
        return (z ^ 1, h, l, r)

    def odd_pair(z, h, l, r):
        return (((z + 1) ^ 1) - 1, h, l, r)

    def far_pair(z, h, l, r):
        return (z - 2, h, l, r) if h == 0 else (z + 2, h, l, r)

    swap_even = moved(tile, even_pair)
    swap_odd = moved(tile, odd_pair)
    far = moved(tile, far_pair)
    other = moved(tile, lambda z, h, l, r: (z, 1 - h, l, r))
    odd_z = (position // 2) % 2 == 1
    up = jnp.where(odd_z, swap_odd, swap_even)
    down = jnp.where(odd_z, swap_even, swap_odd)

    record = jax.ShapeDtypeStruct((3, 16, 128), F32)
    own_fields, other_fields = pl.pallas_call(
        cross_kernel,
        out_shape=(record, record),
        in_specs=[VMEM] * 6,
        out_specs=(VMEM, VMEM),
        scratch_shapes=[pltpu.VMEM((10, 4, 64, 128), F32), pltpu.VMEM((272, 512), F32)],
        compiler_params=pltpu.CompilerParams(vmem_limit_bytes=24 * 2**20),
        name="cross",
    )(tile, other, up, down, far, jnp.asarray(look_table()))

    swapped = moved(other_fields, lambda z, h, l, r: (z, 1 - h, l, r))
    own_beside = moved(own_fields, lambda z, h, l, r: (z, h, 1 - l, r))
    swapped_beside = moved(other_fields, lambda z, h, l, r: (z, 1 - h, 1 - l, r))
    fields = pl.pallas_call(
        choose_kernel,
        out_shape=jax.ShapeDtypeStruct((3, 32, 128), F32),
        in_specs=[SMEM] + [VMEM] * 4,
        out_specs=VMEM,
        compiler_params=pltpu.CompilerParams(vmem_limit_bytes=4 * 2**20),
        name="choose",
    )(pairs, own_fields, swapped, own_beside, swapped_beside)

    core_halo = moved(fields, lambda z, h, l, r: (z, h, l, r ^ 1))
    chip_halo = moved(fields, lambda z, h, l, r: (z, h, l, ((r + 1) ^ 1) - 1))
    filtered, coherence = pl.pallas_call(
        finish_kernel,
        out_shape=(jax.ShapeDtypeStruct((3, 2, 16, 32), F32), jax.ShapeDtypeStruct((3, 16, 32), F32)),
        in_specs=[VMEM] * 10,
        out_specs=(VMEM, VMEM),
        compiler_params=pltpu.CompilerParams(vmem_limit_bytes=24 * 2**20),
        name="finish",
    )(fields, core_halo, chip_halo, *[jnp.asarray(t) for t in tables()])
    return (filtered[None], coherence[None])


def solution(mesh):
    placed = (P("tm", None, "az", "rg"), P("tm", None))
    return jax.shard_map(
        per_device,
        mesh=mesh,
        in_specs=placed,
        out_specs=(P("tm", None, None, "az", "rg"), P("tm", None, "az", "rg")),
        check_vma=False,
    )
```

```python
import math

import jax
import jax.numpy as jnp
import ml_dtypes
import numpy as np
from jax import lax
from jax.experimental import pallas as pl
from jax.experimental.pallas import tpu as pltpu
from jax.sharding import Mesh, PartitionSpec as P

F32 = jnp.float32
BF16 = jnp.bfloat16
EVERY = ("tm", "az", "rg")


def split_table(table):
    high = table.astype(ml_dtypes.bfloat16)
    low = (table - high.astype(np.float64)).astype(ml_dtypes.bfloat16)
    return high, low


def column_tables():
    forward = np.zeros((256, 384))
    back = np.zeros((256, 256))
    steps = np.arange(32)
    taper = np.sin(math.pi * (steps + 0.5) / 32.0) ** 2

    def row_of(field, column):
        if column < 16:
            return 128 + field * 32 + 16 + column
        if column < 48:
            return field * 32 + column - 16
        return 128 + field * 32 + column - 48

    for patch in range(3):
        for j in range(32):
            angle = 2.0 * math.pi * (j * steps % 32) / 32.0
            real, imag = row_of(0, patch * 16 + j), row_of(1, patch * 16 + j)
            at = patch * 32 + steps
            forward[real, at] = np.cos(angle)
            forward[imag, at] = np.sin(angle)
            forward[real, 128 + at] = -np.sin(angle)
            forward[imag, 128 + at] = np.cos(angle)
            column = patch * 16 + j - 16
            if 0 <= column < 32:
                scale = taper[j] / 32.0
                back[at, column] = np.cos(angle) * scale
                back[128 + at, column] = -np.sin(angle) * scale
                back[at, 128 + column] = np.sin(angle) * scale
                back[128 + at, 128 + column] = np.cos(angle) * scale
    for field in range(4):
        for cell in range(32):
            for column in range(cell + 14, cell + 19):
                forward[row_of(field, column), 256 + field * 32 + cell] = 1.0
    return forward, back


def line_tables():
    forward = np.zeros((2, 128, 64))
    window = np.zeros((2, 16, 32))
    back = np.zeros((32, 128))
    steps = np.arange(32)
    taper = np.sin(math.pi * (steps + 0.5) / 32.0) ** 2
    for side in range(2):
        places = {}
        for line in range(16):
            places[16 + line] = line
            places[(32 if side == 0 else 0) + line] = 16 + line
        for patch in range(2):
            for j in range(32):
                row = places.get(patch * 16 + j)
                if row is None:
                    continue
                angle = 2.0 * math.pi * (j * steps % 32) / 32.0
                at = patch * 32 + steps
                forward[side, at, row] = np.cos(angle)
                forward[side, at, 32 + row] = np.sin(angle)
                forward[side, 64 + at, row] = -np.sin(angle)
                forward[side, 64 + at, 32 + row] = np.cos(angle)
        for cell in range(16):
            for line in range(cell + 14, cell + 19):
                if line in places:
                    window[side, cell, places[line]] = 1.0
    for patch in range(2):
        for j in range(32):
            cell = patch * 16 + j - 16
            if 0 <= cell < 16:
                angle = 2.0 * math.pi * (j * steps % 32) / 32.0
                scale = taper[j] / 32.0
                at = patch * 32 + steps
                back[cell, at] = np.cos(angle) * scale
                back[cell, 64 + at] = -np.sin(angle) * scale
                back[16 + cell, at] = np.sin(angle) * scale
                back[16 + cell, 64 + at] = np.cos(angle) * scale
    return forward, window, back


def tables():
    column_forward, column_back = column_tables()
    line_forward, window, line_back = line_tables()
    cf_high, cf_low = split_table(column_forward)
    cb_high, cb_low = split_table(column_back)
    lf_high, lf_low = split_table(line_forward)
    lb_high, lb_low = split_table(line_back)
    return (
        cf_high,
        cf_low,
        np.concatenate([lf_high, lf_high, lf_low], axis=2),
        np.concatenate([window, window], axis=2).astype(ml_dtypes.bfloat16),
        np.concatenate([lb_high, lb_high, lb_low], axis=1),
        cb_high,
        cb_low,
    )


def look_table():
    table = np.zeros((512, 128))
    columns = np.arange(512)
    table[columns, columns // 16] = 1.0 / 64.0
    return table.astype(ml_dtypes.bfloat16)


def halves(values):
    high = values.astype(BF16)
    low = (values - high.astype(F32)).astype(BF16)
    return high, low


def dot(left, right):
    return jnp.dot(left, right, preferred_element_type=F32)


def widened(tiles, wide):
    for index, tile in enumerate(tiles):
        for part in range(2):
            for chunk in range(4):
                at = slice(chunk * 128, chunk * 128 + 128)
                wide[index * 2 + part, chunk] = tile[part, :, at].astype(F32)


def looked_records(couples, count, wide, sums, look):
    number = len(couples)
    for chunk in range(4):
        at = slice(chunk * 128, chunk * 128 + 128)
        totals = [None] * (2 * number + count)
        for line in range(4):
            rows = pl.ds(line, 16, stride=4)
            real = [wide[2 * i, chunk, rows, :] for i in range(count)]
            imag = [wide[2 * i + 1, chunk, rows, :] for i in range(count)]
            terms = []
            for u, v in couples:
                terms.append(real[u] * real[v] + imag[u] * imag[v])
            for u, v in couples:
                terms.append(imag[u] * real[v] - real[u] * imag[v])
            for u in range(count):
                terms.append(real[u] * real[u] + imag[u] * imag[u])
            totals = [t if s is None else s + t for s, t in zip(totals, terms)]
        for index, total in enumerate(totals):
            sums[index * 16 : index * 16 + 16, at] = total
    high, low = halves(sums[...])
    table = look[...]
    looked = dot(high, table) + dot(low, table)
    fields = [looked[i * 16 : i * 16 + 16] for i in range(2 * number + count)]
    power = fields[2 * number :]
    records = []
    for index, (u, v) in enumerate(couples):
        crossed = fields[index] + pltpu.roll(fields[number + index], 32, 1)
        records.append(crossed + pltpu.roll(power[v], 64, 1) + pltpu.roll(power[u], 96, 1))
    return records


def cross_kernel(own, other, up, down, look, own_out, other_out, wide, sums):
    widened((own, other, up, down), wide)
    records = looked_records(((0, 1), (0, 2), (0, 3), (1, 2), (1, 3)), 4, wide, sums, look)
    for index in range(3):
        own_out[index] = records[index]
    for index in range(2):
        other_out[index] = records[3 + index]


def offsets_of(pairs):
    position = lax.axis_index("tm")
    odd = position % 2 == 1
    offset = pairs[...] - position
    return odd, jnp.where(odd, -offset, offset)


def crossed_slots(flipped):
    return (flipped == 3) | (flipped == -1)


def choose_kernel(pairs, own_tile, far_tile, own, swapped, look, out, wide, sums):
    odd, flipped = offsets_of(pairs)
    up = jnp.where(odd, -2, 2)
    widened((own_tile, far_tile), wide)
    (far,) = looked_records(((0, 1),), 2, wide, sums, look)
    third = jnp.where(odd, swapped[1], swapped[0])
    first = jnp.where(odd, swapped[0], swapped[1])
    for slot in range(3):
        at = flipped[:, slot : slot + 1]
        record = jnp.where(at == 1, own[0], far)
        record = jnp.where(at == up, own[1], record)
        record = jnp.where(at == -up, own[2], record)
        record = jnp.where(at == 3, third, record)
        out[slot] = jnp.where(at == -1, first, record)


def finish_kernel(
    pairs,
    fields,
    core_fields,
    chip_fields,
    cf_high,
    cf_low,
    lf,
    window,
    lb,
    cb_high,
    cb_low,
    filtered,
    coherence,
):
    side = lax.axis_index("az")
    column = lax.axis_index("rg")
    core = column % 2
    lane = lax.broadcasted_iota(jnp.int32, (1, 128), 1)
    place = lane % 32
    from_core = (place >= 16) == (core == 1)
    inside = (column > 0) & (column < 7)

    from_chip = jnp.where(inside, chip_fields[...].reshape(96, 128), 0.0)
    halo = jnp.where(from_core, core_fields[...].reshape(96, 128), from_chip)
    values = jnp.concatenate([fields[...].reshape(96, 128), halo], axis=1)
    high, low = halves(values)
    table = cf_high[...]
    mixed = dot(high, table) + dot(low, table) + dot(high, cf_low[...])
    crossed = crossed_slots(offsets_of(pairs)[1])
    rows = []
    for slot in range(3):
        first, second = mixed[16 * slot : 16 * slot + 16], mixed[48 + 16 * slot : 64 + 16 * slot]
        turn = crossed[:, slot : slot + 1]
        rows.append(jnp.concatenate([jnp.where(turn, second, first), jnp.where(turn, first, second)], axis=0))
    real = jnp.concatenate([r[:, 0:128] for r in rows], axis=1)
    imag = jnp.concatenate([r[:, 128:256] for r in rows], axis=1)
    sums = jnp.concatenate([r[:, 256:384] for r in rows], axis=1)
    high, low = halves(jnp.concatenate([real, imag], axis=0))
    spectrum = dot(lf[side], jnp.concatenate([high, low, high], axis=0))
    spec_real, spec_imag = spectrum[0:64], spectrum[64:128]
    power = jnp.sqrt(spec_real * spec_real + spec_imag * spec_imag)

    def turned(block, by):
        away = pltpu.roll(block, by % 128, 1)
        wrapped = pltpu.roll(block, (by - 32) % 128, 1)
        if by > 0:
            return jnp.where(place < by, wrapped, away)
        wrapped = pltpu.roll(block, (by + 32) % 128, 1)
        return jnp.where(place >= 32 + by, wrapped, away)

    smoothed = []
    for patch in range(2):
        for slot in range(3):
            block = power[32 * patch : 32 * patch + 32, 128 * slot : 128 * slot + 128]
            block = block + pltpu.roll(block, 1, 0) + pltpu.roll(block, 31, 0)
            block = block + turned(block, 1) + turned(block, -1)
            smoothed.append(block / 9.0)
    largest = jnp.concatenate([jnp.max(b, axis=0, keepdims=True) for b in smoothed] + [jnp.zeros((2, 128), F32)], axis=0)
    for by in (1, 2, 4, 8, 16):
        largest = jnp.maximum(largest, turned(largest, by))
    scale = 1.0 / (jnp.sqrt(largest) + 1e-06)
    weights = [jnp.sqrt(b) * scale[i : i + 1] for i, b in enumerate(smoothed)]
    weights = jnp.concatenate(
        [jnp.concatenate(weights[0:3], axis=1), jnp.concatenate(weights[3:6], axis=1)], axis=0
    )
    high, low = halves(jnp.concatenate([spec_real * weights, spec_imag * weights], axis=0))
    lines = dot(lb[...], jnp.concatenate([high, low, high], axis=0))
    stacked = jnp.concatenate(
        [
            jnp.concatenate([lines[0:16, 128 * s : 128 * s + 128], lines[16:32, 128 * s : 128 * s + 128]], axis=1)
            for s in range(3)
        ],
        axis=0,
    )
    high, low = halves(stacked)
    table = cb_high[...]
    result = dot(high, table) + dot(low, table) + dot(high, cb_low[...])
    for slot in range(3):
        filtered[slot, 0] = result[16 * slot : 16 * slot + 16, 0:32]
        filtered[slot, 1] = result[16 * slot : 16 * slot + 16, 128:160]

    high, low = halves(sums)
    totals = dot(window[side], jnp.concatenate([high, low], axis=0))
    for slot in range(3):
        total = totals[:, 128 * slot : 128 * slot + 128]
        square = total * total
        square = square + pltpu.roll(square, 96, 1)
        product = total * pltpu.roll(total, 96, 1)
        product = pltpu.roll(product, 64, 1)
        coherence[slot] = (jnp.sqrt(square) / jnp.sqrt(product))[:, 0:32]


VMEM = pl.BlockSpec(memory_space=pltpu.VMEM)


def moved(value, where):
    pairs = []
    for z in range(8):
        for yh in range(2):
            for yl in range(2):
                for r in range(8):
                    tz, th, tl, tr = where(z, yh, yl, r)
                    pairs.append((((z * 2 + yh) * 2 + yl) * 8 + r, ((tz % 8 * 2 + th) * 2 + tl) * 8 + tr % 8))
    return lax.ppermute(value, EVERY, pairs)


def per_device(slc, pairs):
    tile = slc[0]
    position = lax.axis_index("tm")

    def even_pair(z, h, l, r):
        return (z ^ 1, h, l, r)

    def odd_pair(z, h, l, r):
        return (((z + 1) ^ 1) - 1, h, l, r)

    def far_pair(z, h, l, r):
        return (z - 2, 1, l, r) if h == 0 else (z + 2, 0, l, r)

    far = moved(tile, far_pair)
    swap_even = moved(tile, even_pair)
    swap_odd = moved(tile, odd_pair)
    other = moved(tile, lambda z, h, l, r: (z, 1 - h, l, r))
    odd_z = (position // 2) % 2 == 1
    up = jnp.where(odd_z, swap_odd, swap_even)
    down = jnp.where(odd_z, swap_even, swap_odd)
    look = jnp.asarray(look_table())

    own_fields, other_fields = pl.pallas_call(
        cross_kernel,
        out_shape=(jax.ShapeDtypeStruct((3, 16, 128), F32), jax.ShapeDtypeStruct((2, 16, 128), F32)),
        in_specs=[VMEM] * 5,
        out_specs=(VMEM, VMEM),
        scratch_shapes=[pltpu.VMEM((8, 4, 64, 128), F32), pltpu.VMEM((224, 512), F32)],
        compiler_params=pltpu.CompilerParams(vmem_limit_bytes=16 * 2**20),
        name="cross",
    )(tile, other, up, down, look)
    swapped = moved(other_fields, lambda z, h, l, r: (z, 1 - h, 1 - l, r))
    fields = pl.pallas_call(
        choose_kernel,
        out_shape=jax.ShapeDtypeStruct((3, 16, 128), F32),
        in_specs=[VMEM] * 6,
        out_specs=VMEM,
        scratch_shapes=[pltpu.VMEM((4, 4, 64, 128), F32), pltpu.VMEM((64, 512), F32)],
        compiler_params=pltpu.CompilerParams(vmem_limit_bytes=16 * 2**20),
        name="choose",
    )(pairs, tile, far, own_fields, swapped, look)

    def to_core(value):
        return moved(value, lambda z, h, l, r: (z, h, l, r ^ 1))

    def to_chip(value):
        return moved(value, lambda z, h, l, r: (z, h, l, ((r + 1) ^ 1) - 1))

    beside = moved(fields, lambda z, h, l, r: (z, h, 1 - l, r))
    fields = jnp.concatenate([fields, beside], axis=0)
    core_fields = to_core(fields)
    chip_fields = to_chip(fields)
    filtered, coherence = pl.pallas_call(
        finish_kernel,
        out_shape=(jax.ShapeDtypeStruct((3, 2, 16, 32), F32), jax.ShapeDtypeStruct((3, 16, 32), F32)),
        in_specs=[VMEM] * 11,
        out_specs=(VMEM, VMEM),
        compiler_params=pltpu.CompilerParams(vmem_limit_bytes=24 * 2**20),
        name="finish",
    )(
        pairs,
        fields,
        core_fields,
        chip_fields,
        *[jnp.asarray(t) for t in tables()],
    )
    return (filtered[None], coherence[None])


def solution(mesh):
    placed = (P("tm", None, "az", "rg"), P("tm", None))
    return jax.shard_map(
        per_device,
        mesh=mesh,
        in_specs=placed,
        out_specs=(P("tm", None, None, "az", "rg"), P("tm", None, "az", "rg")),
        check_vma=False,
    )
```

```python
import math

import jax
import jax.numpy as jnp
import ml_dtypes
import numpy as np
from jax import lax
from jax.experimental import pallas as pl
from jax.experimental.pallas import tpu as pltpu
from jax.sharding import Mesh, PartitionSpec as P

F32 = jnp.float32
BF16 = jnp.bfloat16
EVERY = ("tm", "az", "rg")


def split_table(table):
    high = table.astype(ml_dtypes.bfloat16)
    low = (table - high.astype(np.float64)).astype(ml_dtypes.bfloat16)
    return high, low


def column_tables():
    forward = np.zeros((256, 384))
    back = np.zeros((256, 256))
    steps = np.arange(32)
    taper = np.sin(math.pi * (steps + 0.5) / 32.0) ** 2

    def row_of(field, column):
        if column < 16:
            return 128 + field * 32 + 16 + column
        if column < 48:
            return field * 32 + column - 16
        return 128 + field * 32 + column - 48

    for patch in range(3):
        for j in range(32):
            angle = 2.0 * math.pi * (j * steps % 32) / 32.0
            real, imag = row_of(0, patch * 16 + j), row_of(1, patch * 16 + j)
            at = patch * 32 + steps
            forward[real, at] = np.cos(angle)
            forward[imag, at] = np.sin(angle)
            forward[real, 128 + at] = -np.sin(angle)
            forward[imag, 128 + at] = np.cos(angle)
            column = patch * 16 + j - 16
            if 0 <= column < 32:
                scale = taper[j] / 32.0
                back[at, column] = np.cos(angle) * scale
                back[128 + at, column] = -np.sin(angle) * scale
                back[at, 128 + column] = np.sin(angle) * scale
                back[128 + at, 128 + column] = np.cos(angle) * scale
    for field in range(4):
        for cell in range(32):
            for column in range(cell + 14, cell + 19):
                forward[row_of(field, column), 256 + field * 32 + cell] = 1.0
    return forward, back


def line_tables():
    forward = np.zeros((2, 128, 64))
    window = np.zeros((2, 16, 32))
    back = np.zeros((32, 128))
    steps = np.arange(32)
    taper = np.sin(math.pi * (steps + 0.5) / 32.0) ** 2
    for side in range(2):
        places = {}
        for line in range(16):
            places[16 + line] = line
            places[(32 if side == 0 else 0) + line] = 16 + line
        for patch in range(2):
            for j in range(32):
                row = places.get(patch * 16 + j)
                if row is None:
                    continue
                angle = 2.0 * math.pi * (j * steps % 32) / 32.0
                at = patch * 32 + steps
                forward[side, at, row] = np.cos(angle)
                forward[side, at, 32 + row] = np.sin(angle)
                forward[side, 64 + at, row] = -np.sin(angle)
                forward[side, 64 + at, 32 + row] = np.cos(angle)
        for cell in range(16):
            for line in range(cell + 14, cell + 19):
                if line in places:
                    window[side, cell, places[line]] = 1.0
    for patch in range(2):
        for j in range(32):
            cell = patch * 16 + j - 16
            if 0 <= cell < 16:
                angle = 2.0 * math.pi * (j * steps % 32) / 32.0
                scale = taper[j] / 32.0
                at = patch * 32 + steps
                back[cell, at] = np.cos(angle) * scale
                back[cell, 64 + at] = -np.sin(angle) * scale
                back[16 + cell, at] = np.sin(angle) * scale
                back[16 + cell, 64 + at] = np.cos(angle) * scale
    return forward, window, back


def tables():
    column_forward, column_back = column_tables()
    line_forward, window, line_back = line_tables()
    cf_high, cf_low = split_table(column_forward)
    cb_high, cb_low = split_table(column_back)
    lf_high, lf_low = split_table(line_forward)
    lb_high, lb_low = split_table(line_back)
    return (
        cf_high,
        cf_low,
        np.concatenate([lf_high, lf_high, lf_low], axis=2),
        np.concatenate([window, window], axis=2).astype(ml_dtypes.bfloat16),
        np.concatenate([lb_high, lb_high, lb_low], axis=1),
        cb_high,
        cb_low,
    )


def look_table():
    table = np.zeros((512, 128))
    columns = np.arange(512)
    table[columns, columns // 16] = 1.0 / 64.0
    return table.astype(ml_dtypes.bfloat16)


def halves(values):
    high = values.astype(BF16)
    low = (values - high.astype(F32)).astype(BF16)
    return high, low


def dot(left, right):
    return jnp.dot(left, right, preferred_element_type=F32)


def widened(tiles, wide):
    for index, tile in enumerate(tiles):
        for part in range(2):
            for chunk in range(4):
                at = slice(chunk * 128, chunk * 128 + 128)
                wide[index * 2 + part, chunk] = tile[part, :, at].astype(F32)


def looked_records(couples, count, wide, sums, look):
    number = len(couples)
    for chunk in range(4):
        at = slice(chunk * 128, chunk * 128 + 128)
        totals = [None] * (2 * number + count)
        for line in range(4):
            rows = pl.ds(line, 16, stride=4)
            real = [wide[2 * i, chunk, rows, :] for i in range(count)]
            imag = [wide[2 * i + 1, chunk, rows, :] for i in range(count)]
            terms = []
            for u, v in couples:
                terms.append(real[u] * real[v] + imag[u] * imag[v])
            for u, v in couples:
                terms.append(imag[u] * real[v] - real[u] * imag[v])
            for u in range(count):
                terms.append(real[u] * real[u] + imag[u] * imag[u])
            totals = [t if s is None else s + t for s, t in zip(totals, terms)]
        for index, total in enumerate(totals):
            sums[index * 16 : index * 16 + 16, at] = total
    high, low = halves(sums[...])
    table = look[...]
    looked = dot(high, table) + dot(low, table)
    fields = [looked[i * 16 : i * 16 + 16] for i in range(2 * number + count)]
    power = fields[2 * number :]
    records = []
    for index, (u, v) in enumerate(couples):
        crossed = fields[index] + pltpu.roll(fields[number + index], 32, 1)
        records.append(crossed + pltpu.roll(power[v], 64, 1) + pltpu.roll(power[u], 96, 1))
    return records


def cross_kernel(own, other, up, down, look, own_out, other_out, wide, sums):
    widened((own, other, up, down), wide)
    records = looked_records(((0, 1), (0, 2), (0, 3), (1, 2), (1, 3)), 4, wide, sums, look)
    for index in range(3):
        own_out[index] = records[index]
    for index in range(2):
        other_out[index] = records[3 + index]


def offsets_of(pairs):
    position = lax.axis_index("tm")
    odd = position % 2 == 1
    offset = pairs[...] - position
    return odd, jnp.where(odd, -offset, offset)


def crossed_slots(flipped):
    return (flipped == 3) | (flipped == -1)


def choose_kernel(pairs, own_tile, far_tile, own, swapped, look, out, wide, sums):
    odd, flipped = offsets_of(pairs)
    up = jnp.where(odd, -2, 2)
    widened((own_tile, far_tile), wide)
    (far,) = looked_records(((0, 1),), 2, wide, sums, look)
    third = jnp.where(odd, swapped[1], swapped[0])
    first = jnp.where(odd, swapped[0], swapped[1])
    for slot in range(3):
        at = flipped[:, slot : slot + 1]
        record = jnp.where(at == 1, own[0], far)
        record = jnp.where(at == up, own[1], record)
        record = jnp.where(at == -up, own[2], record)
        record = jnp.where(at == 3, third, record)
        out[slot] = jnp.where(at == -1, first, record)


def finish_kernel(
    pairs,
    fields,
    core_fields,
    chip_fields,
    cf_high,
    cf_low,
    lf,
    window,
    lb,
    cb_high,
    cb_low,
    filtered,
    coherence,
):
    side = lax.axis_index("az")
    column = lax.axis_index("rg")
    core = column % 2
    lane = lax.broadcasted_iota(jnp.int32, (1, 128), 1)
    place = lane % 32
    from_core = (place >= 16) == (core == 1)
    inside = (column > 0) & (column < 7)

    from_chip = jnp.where(inside, chip_fields[...].reshape(96, 128), 0.0)
    halo = jnp.where(from_core, core_fields[...].reshape(96, 128), from_chip)
    values = jnp.concatenate([fields[...].reshape(96, 128), halo], axis=1)
    high, low = halves(values)
    table = cf_high[...]
    mixed = dot(high, table) + dot(low, table) + dot(high, cf_low[...])
    crossed = crossed_slots(offsets_of(pairs)[1])
    rows = []
    for slot in range(3):
        first, second = mixed[16 * slot : 16 * slot + 16], mixed[48 + 16 * slot : 64 + 16 * slot]
        turn = crossed[:, slot : slot + 1]
        rows.append(jnp.concatenate([jnp.where(turn, second, first), jnp.where(turn, first, second)], axis=0))
    real = jnp.concatenate([r[:, 0:128] for r in rows], axis=1)
    imag = jnp.concatenate([r[:, 128:256] for r in rows], axis=1)
    sums = jnp.concatenate([r[:, 256:384] for r in rows], axis=1)
    high, low = halves(jnp.concatenate([real, imag], axis=0))
    spectrum = dot(lf[side], jnp.concatenate([high, low, high], axis=0))
    spec_real, spec_imag = spectrum[0:64], spectrum[64:128]
    power = jnp.sqrt(spec_real * spec_real + spec_imag * spec_imag)

    def turned(block, by):
        away = pltpu.roll(block, by % 128, 1)
        wrapped = pltpu.roll(block, (by - 32) % 128, 1)
        if by > 0:
            return jnp.where(place < by, wrapped, away)
        wrapped = pltpu.roll(block, (by + 32) % 128, 1)
        return jnp.where(place >= 32 + by, wrapped, away)

    smoothed = []
    for patch in range(2):
        for slot in range(3):
            block = power[32 * patch : 32 * patch + 32, 128 * slot : 128 * slot + 128]
            block = block + pltpu.roll(block, 1, 0) + pltpu.roll(block, 31, 0)
            block = block + turned(block, 1) + turned(block, -1)
            smoothed.append(block / 9.0)
    largest = jnp.concatenate([jnp.max(b, axis=0, keepdims=True) for b in smoothed] + [jnp.zeros((2, 128), F32)], axis=0)
    for by in (1, 2, 4, 8, 16):
        largest = jnp.maximum(largest, turned(largest, by))
    scale = 1.0 / (jnp.sqrt(largest) + 1e-06)
    weights = [jnp.sqrt(b) * scale[i : i + 1] for i, b in enumerate(smoothed)]
    weights = jnp.concatenate(
        [jnp.concatenate(weights[0:3], axis=1), jnp.concatenate(weights[3:6], axis=1)], axis=0
    )
    high, low = halves(jnp.concatenate([spec_real * weights, spec_imag * weights], axis=0))
    lines = dot(lb[...], jnp.concatenate([high, low, high], axis=0))
    stacked = jnp.concatenate(
        [
            jnp.concatenate([lines[0:16, 128 * s : 128 * s + 128], lines[16:32, 128 * s : 128 * s + 128]], axis=1)
            for s in range(3)
        ],
        axis=0,
    )
    high, low = halves(stacked)
    table = cb_high[...]
    result = dot(high, table) + dot(low, table) + dot(high, cb_low[...])
    for slot in range(3):
        filtered[slot, 0] = result[16 * slot : 16 * slot + 16, 0:32]
        filtered[slot, 1] = result[16 * slot : 16 * slot + 16, 128:160]

    high, low = halves(sums)
    totals = dot(window[side], jnp.concatenate([high, low], axis=0))
    for slot in range(3):
        total = totals[:, 128 * slot : 128 * slot + 128]
        square = total * total
        square = square + pltpu.roll(square, 96, 1)
        product = total * pltpu.roll(total, 96, 1)
        product = pltpu.roll(product, 64, 1)
        coherence[slot] = (jnp.sqrt(square) / jnp.sqrt(product))[:, 0:32]


VMEM = pl.BlockSpec(memory_space=pltpu.VMEM)


def moved(value, where):
    pairs = []
    for z in range(8):
        for yh in range(2):
            for yl in range(2):
                for r in range(8):
                    tz, th, tl, tr = where(z, yh, yl, r)
                    if not 0 <= tz < 8:
                        tz, th, tl, tr = z, yh, yl, r ^ 1
                    if not 0 <= tr < 8:
                        tz, th, tl, tr = z, yh, 1 - yl, r
                    pairs.append((((z * 2 + yh) * 2 + yl) * 8 + r, ((tz * 2 + th) * 2 + tl) * 8 + tr))
    return lax.ppermute(value, EVERY, pairs)


def per_device(slc, pairs):
    tile = slc[0]
    position = lax.axis_index("tm")

    def even_pair(z, h, l, r):
        return (z ^ 1, h, l, r)

    def odd_pair(z, h, l, r):
        return (((z + 1) ^ 1) - 1, h, l, r)

    def far_pair(z, h, l, r):
        return (z - 2, 1, l, r) if h == 0 else (z + 2, 0, l, r)

    far = moved(tile, far_pair)
    swap_even = moved(tile, even_pair)
    swap_odd = moved(tile, odd_pair)
    other = moved(tile, lambda z, h, l, r: (z, 1 - h, l, r))
    odd_z = (position // 2) % 2 == 1
    up = jnp.where(odd_z, swap_odd, swap_even)
    down = jnp.where(odd_z, swap_even, swap_odd)
    look = jnp.asarray(look_table())

    own_fields, other_fields = pl.pallas_call(
        cross_kernel,
        out_shape=(jax.ShapeDtypeStruct((3, 16, 128), F32), jax.ShapeDtypeStruct((2, 16, 128), F32)),
        in_specs=[VMEM] * 5,
        out_specs=(VMEM, VMEM),
        scratch_shapes=[pltpu.VMEM((8, 4, 64, 128), F32), pltpu.VMEM((224, 512), F32)],
        compiler_params=pltpu.CompilerParams(vmem_limit_bytes=16 * 2**20),
        name="cross",
    )(tile, other, up, down, look)
    swapped = moved(other_fields, lambda z, h, l, r: (z, 1 - h, 1 - l, r))
    fields = pl.pallas_call(
        choose_kernel,
        out_shape=jax.ShapeDtypeStruct((3, 16, 128), F32),
        in_specs=[VMEM] * 6,
        out_specs=VMEM,
        scratch_shapes=[pltpu.VMEM((4, 4, 64, 128), F32), pltpu.VMEM((64, 512), F32)],
        compiler_params=pltpu.CompilerParams(vmem_limit_bytes=16 * 2**20),
        name="choose",
    )(pairs, tile, far, own_fields, swapped, look)

    def to_core(value):
        return moved(value, lambda z, h, l, r: (z, h, l, r ^ 1))

    def to_chip(value):
        return moved(value, lambda z, h, l, r: (z, h, l, ((r + 1) ^ 1) - 1))

    beside = moved(fields, lambda z, h, l, r: (z, h, 1 - l, r))
    fields = jnp.concatenate([fields, beside], axis=0)
    core_fields = to_core(fields)
    chip_fields = to_chip(fields)
    filtered, coherence = pl.pallas_call(
        finish_kernel,
        out_shape=(jax.ShapeDtypeStruct((3, 2, 16, 32), F32), jax.ShapeDtypeStruct((3, 16, 32), F32)),
        in_specs=[VMEM] * 11,
        out_specs=(VMEM, VMEM),
        compiler_params=pltpu.CompilerParams(vmem_limit_bytes=24 * 2**20),
        name="finish",
    )(
        pairs,
        fields,
        core_fields,
        chip_fields,
        *[jnp.asarray(t) for t in tables()],
    )
    return (filtered[None], coherence[None])


def solution(mesh):
    placed = (P("tm", None, "az", "rg"), P("tm", None))
    return jax.shard_map(
        per_device,
        mesh=mesh,
        in_specs=placed,
        out_specs=(P("tm", None, None, "az", "rg"), P("tm", None, "az", "rg")),
        check_vma=False,
    )
```

```python
import math

import jax
import jax.numpy as jnp
import ml_dtypes
import numpy as np
from jax import lax
from jax.experimental import pallas as pl
from jax.experimental.pallas import tpu as pltpu
from jax.sharding import Mesh, PartitionSpec as P

F32 = jnp.float32
BF16 = jnp.bfloat16
EVERY = ("tm", "az", "rg")


def split_table(table):
    high = table.astype(ml_dtypes.bfloat16)
    low = (table - high.astype(np.float64)).astype(ml_dtypes.bfloat16)
    return high, low


def column_tables():
    forward = np.zeros((256, 384))
    back = np.zeros((256, 256))
    steps = np.arange(32)
    taper = np.sin(math.pi * (steps + 0.5) / 32.0) ** 2

    def row_of(field, column):
        if column < 16:
            return 128 + field * 32 + 16 + column
        if column < 48:
            return field * 32 + column - 16
        return 128 + field * 32 + column - 48

    for patch in range(3):
        for j in range(32):
            angle = 2.0 * math.pi * (j * steps % 32) / 32.0
            real, imag = row_of(0, patch * 16 + j), row_of(1, patch * 16 + j)
            at = patch * 32 + steps
            forward[real, at] = np.cos(angle)
            forward[imag, at] = np.sin(angle)
            forward[real, 128 + at] = -np.sin(angle)
            forward[imag, 128 + at] = np.cos(angle)
            column = patch * 16 + j - 16
            if 0 <= column < 32:
                scale = taper[j] / 32.0
                back[at, column] = np.cos(angle) * scale
                back[128 + at, column] = -np.sin(angle) * scale
                back[at, 128 + column] = np.sin(angle) * scale
                back[128 + at, 128 + column] = np.cos(angle) * scale
    for field in range(4):
        for cell in range(32):
            for column in range(cell + 14, cell + 19):
                forward[row_of(field, column), 256 + field * 32 + cell] = 1.0
    return forward, back


def line_tables():
    forward = np.zeros((2, 128, 64))
    window = np.zeros((2, 16, 32))
    back = np.zeros((32, 128))
    steps = np.arange(32)
    taper = np.sin(math.pi * (steps + 0.5) / 32.0) ** 2
    for side in range(2):
        places = {}
        for line in range(16):
            places[16 + line] = line
            places[(32 if side == 0 else 0) + line] = 16 + line
        for patch in range(2):
            for j in range(32):
                row = places.get(patch * 16 + j)
                if row is None:
                    continue
                angle = 2.0 * math.pi * (j * steps % 32) / 32.0
                at = patch * 32 + steps
                forward[side, at, row] = np.cos(angle)
                forward[side, at, 32 + row] = np.sin(angle)
                forward[side, 64 + at, row] = -np.sin(angle)
                forward[side, 64 + at, 32 + row] = np.cos(angle)
        for cell in range(16):
            for line in range(cell + 14, cell + 19):
                if line in places:
                    window[side, cell, places[line]] = 1.0
    for patch in range(2):
        for j in range(32):
            cell = patch * 16 + j - 16
            if 0 <= cell < 16:
                angle = 2.0 * math.pi * (j * steps % 32) / 32.0
                scale = taper[j] / 32.0
                at = patch * 32 + steps
                back[cell, at] = np.cos(angle) * scale
                back[cell, 64 + at] = -np.sin(angle) * scale
                back[16 + cell, at] = np.sin(angle) * scale
                back[16 + cell, 64 + at] = np.cos(angle) * scale
    return forward, window, back


def tables():
    column_forward, column_back = column_tables()
    line_forward, window, line_back = line_tables()
    cf_high, cf_low = split_table(column_forward)
    cb_high, cb_low = split_table(column_back)
    lf_high, lf_low = split_table(line_forward)
    lb_high, lb_low = split_table(line_back)
    return (
        cf_high,
        cf_low,
        np.concatenate([lf_high, lf_high, lf_low], axis=2),
        np.concatenate([window, window], axis=2).astype(ml_dtypes.bfloat16),
        np.concatenate([lb_high, lb_high, lb_low], axis=1),
        cb_high,
        cb_low,
    )


def look_table():
    table = np.zeros((512, 128))
    columns = np.arange(512)
    table[columns, columns // 16] = 1.0 / 64.0
    return table.astype(ml_dtypes.bfloat16)


def halves(values):
    high = values.astype(BF16)
    low = (values - high.astype(F32)).astype(BF16)
    return high, low


def dot(left, right):
    return jnp.dot(left, right, preferred_element_type=F32)


def widened(tiles, wide):
    for index, tile in enumerate(tiles):
        for part in range(2):
            for chunk in range(4):
                at = slice(chunk * 128, chunk * 128 + 128)
                wide[index * 2 + part, chunk] = tile[part, :, at].astype(F32)


def looked_records(couples, count, wide, sums, look):
    number = len(couples)
    for chunk in range(4):
        at = slice(chunk * 128, chunk * 128 + 128)
        totals = [None] * (2 * number + count)
        for line in range(4):
            rows = pl.ds(line, 16, stride=4)
            real = [wide[2 * i, chunk, rows, :] for i in range(count)]
            imag = [wide[2 * i + 1, chunk, rows, :] for i in range(count)]
            terms = []
            for u, v in couples:
                terms.append(real[u] * real[v] + imag[u] * imag[v])
            for u, v in couples:
                terms.append(imag[u] * real[v] - real[u] * imag[v])
            for u in range(count):
                terms.append(real[u] * real[u] + imag[u] * imag[u])
            totals = [t if s is None else s + t for s, t in zip(totals, terms)]
        for index, total in enumerate(totals):
            sums[index * 16 : index * 16 + 16, at] = total
    high, low = halves(sums[...])
    table = look[...]
    looked = dot(high, table) + dot(low, table)
    fields = [looked[i * 16 : i * 16 + 16] for i in range(2 * number + count)]
    power = fields[2 * number :]
    records = []
    for index, (u, v) in enumerate(couples):
        crossed = fields[index] + pltpu.roll(fields[number + index], 32, 1)
        records.append(crossed + pltpu.roll(power[v], 64, 1) + pltpu.roll(power[u], 96, 1))
    return records


def cross_kernel(own, other, up, down, look, own_out, other_out, wide, sums):
    widened((own, other, up, down), wide)
    records = looked_records(((0, 1), (0, 2), (0, 3), (1, 2), (1, 3)), 4, wide, sums, look)
    for index in range(3):
        own_out[index] = records[index]
    for index in range(2):
        other_out[index] = records[3 + index]


def offsets_of(pairs):
    position = lax.axis_index("tm")
    odd = position % 2 == 1
    offset = pairs[...] - position
    return odd, jnp.where(odd, -offset, offset)


def crossed_slots(flipped):
    return (flipped == 3) | (flipped == -1)


def choose_kernel(pairs, own_tile, far_tile, own, swapped, look, out, wide, sums):
    odd, flipped = offsets_of(pairs)
    up = jnp.where(odd, -2, 2)
    widened((own_tile, far_tile), wide)
    (far,) = looked_records(((0, 1),), 2, wide, sums, look)
    third = jnp.where(odd, swapped[1], swapped[0])
    first = jnp.where(odd, swapped[0], swapped[1])
    for slot in range(3):
        at = flipped[:, slot : slot + 1]
        record = jnp.where(at == 1, own[0], far)
        record = jnp.where(at == up, own[1], record)
        record = jnp.where(at == -up, own[2], record)
        record = jnp.where(at == 3, third, record)
        out[slot] = jnp.where(at == -1, first, record)


def finish_kernel(
    pairs,
    fields,
    core_fields,
    chip_fields,
    cf_high,
    cf_low,
    lf,
    window,
    lb,
    cb_high,
    cb_low,
    filtered,
    coherence,
):
    side = lax.axis_index("az")
    column = lax.axis_index("rg")
    core = column % 2
    lane = lax.broadcasted_iota(jnp.int32, (1, 128), 1)
    place = lane % 32
    from_core = (place >= 16) == (core == 1)
    inside = (column > 0) & (column < 7)

    from_chip = jnp.where(inside, chip_fields[...].reshape(96, 128), 0.0)
    halo = jnp.where(from_core, core_fields[...].reshape(96, 128), from_chip)
    values = jnp.concatenate([fields[...].reshape(96, 128), halo], axis=1)
    high, low = halves(values)
    table = cf_high[...]
    mixed = dot(high, table) + dot(low, table) + dot(high, cf_low[...])
    crossed = crossed_slots(offsets_of(pairs)[1])
    rows = []
    for slot in range(3):
        first, second = mixed[16 * slot : 16 * slot + 16], mixed[48 + 16 * slot : 64 + 16 * slot]
        turn = crossed[:, slot : slot + 1]
        rows.append(jnp.concatenate([jnp.where(turn, second, first), jnp.where(turn, first, second)], axis=0))
    real = jnp.concatenate([r[:, 0:128] for r in rows], axis=1)
    imag = jnp.concatenate([r[:, 128:256] for r in rows], axis=1)
    sums = jnp.concatenate([r[:, 256:384] for r in rows], axis=1)
    high, low = halves(jnp.concatenate([real, imag], axis=0))
    spectrum = dot(lf[side], jnp.concatenate([high, low, high], axis=0))
    spec_real, spec_imag = spectrum[0:64], spectrum[64:128]
    power = jnp.sqrt(spec_real * spec_real + spec_imag * spec_imag)

    def turned(block, by):
        away = pltpu.roll(block, by % 128, 1)
        wrapped = pltpu.roll(block, (by - 32) % 128, 1)
        if by > 0:
            return jnp.where(place < by, wrapped, away)
        wrapped = pltpu.roll(block, (by + 32) % 128, 1)
        return jnp.where(place >= 32 + by, wrapped, away)

    smoothed = []
    for patch in range(2):
        for slot in range(3):
            block = power[32 * patch : 32 * patch + 32, 128 * slot : 128 * slot + 128]
            block = block + pltpu.roll(block, 1, 0) + pltpu.roll(block, 31, 0)
            block = block + turned(block, 1) + turned(block, -1)
            smoothed.append(block / 9.0)
    largest = jnp.concatenate([jnp.max(b, axis=0, keepdims=True) for b in smoothed] + [jnp.zeros((2, 128), F32)], axis=0)
    groups = [jnp.max(jnp.where(lane // 32 == g, largest, 0.0), axis=1, keepdims=True) for g in range(3)]
    largest = jnp.where(lane < 32, groups[0], jnp.where(lane < 64, groups[1], groups[2]))
    scale = 1.0 / (jnp.sqrt(largest) + 1e-06)
    weights = [jnp.sqrt(b) * scale[i : i + 1] for i, b in enumerate(smoothed)]
    weights = jnp.concatenate(
        [jnp.concatenate(weights[0:3], axis=1), jnp.concatenate(weights[3:6], axis=1)], axis=0
    )
    high, low = halves(jnp.concatenate([spec_real * weights, spec_imag * weights], axis=0))
    lines = dot(lb[...], jnp.concatenate([high, low, high], axis=0))
    stacked = jnp.concatenate(
        [
            jnp.concatenate([lines[0:16, 128 * s : 128 * s + 128], lines[16:32, 128 * s : 128 * s + 128]], axis=1)
            for s in range(3)
        ],
        axis=0,
    )
    high, low = halves(stacked)
    table = cb_high[...]
    result = dot(high, table) + dot(low, table) + dot(high, cb_low[...])
    for slot in range(3):
        filtered[slot, 0] = result[16 * slot : 16 * slot + 16, 0:32]
        filtered[slot, 1] = result[16 * slot : 16 * slot + 16, 128:160]

    high, low = halves(sums)
    totals = dot(window[side], jnp.concatenate([high, low], axis=0))
    for slot in range(3):
        total = totals[:, 128 * slot : 128 * slot + 128]
        square = total * total
        square = square + pltpu.roll(square, 96, 1)
        product = total * pltpu.roll(total, 96, 1)
        product = pltpu.roll(product, 64, 1)
        coherence[slot] = (jnp.sqrt(square) / jnp.sqrt(product))[:, 0:32]


VMEM = pl.BlockSpec(memory_space=pltpu.VMEM)


def moved(value, where):
    pairs = []
    for z in range(8):
        for yh in range(2):
            for yl in range(2):
                for r in range(8):
                    tz, th, tl, tr = where(z, yh, yl, r)
                    if not 0 <= tz < 8:
                        tz, th, tl, tr = z, yh, yl, r ^ 1
                    if not 0 <= tr < 8:
                        tz, th, tl, tr = z, yh, 1 - yl, r
                    pairs.append((((z * 2 + yh) * 2 + yl) * 8 + r, ((tz * 2 + th) * 2 + tl) * 8 + tr))
    return lax.ppermute(value, EVERY, pairs)


def per_device(slc, pairs):
    tile = slc[0]
    position = lax.axis_index("tm")

    def even_pair(z, h, l, r):
        return (z ^ 1, h, l, r)

    def odd_pair(z, h, l, r):
        return (((z + 1) ^ 1) - 1, h, l, r)

    def far_pair(z, h, l, r):
        return (z - 2, 1, l, r) if h == 0 else (z + 2, 0, l, r)

    far = moved(tile, far_pair)
    swap_even = moved(tile, even_pair)
    swap_odd = moved(tile, odd_pair)
    other = moved(tile, lambda z, h, l, r: (z, 1 - h, l, r))
    odd_z = (position // 2) % 2 == 1
    up = jnp.where(odd_z, swap_odd, swap_even)
    down = jnp.where(odd_z, swap_even, swap_odd)
    look = jnp.asarray(look_table())

    own_fields, other_fields = pl.pallas_call(
        cross_kernel,
        out_shape=(jax.ShapeDtypeStruct((3, 16, 128), F32), jax.ShapeDtypeStruct((2, 16, 128), F32)),
        in_specs=[VMEM] * 5,
        out_specs=(VMEM, VMEM),
        scratch_shapes=[pltpu.VMEM((8, 4, 64, 128), F32), pltpu.VMEM((224, 512), F32)],
        compiler_params=pltpu.CompilerParams(vmem_limit_bytes=16 * 2**20),
        name="cross",
    )(tile, other, up, down, look)
    swapped = moved(other_fields, lambda z, h, l, r: (z, 1 - h, 1 - l, r))
    fields = pl.pallas_call(
        choose_kernel,
        out_shape=jax.ShapeDtypeStruct((3, 16, 128), F32),
        in_specs=[VMEM] * 6,
        out_specs=VMEM,
        scratch_shapes=[pltpu.VMEM((4, 4, 64, 128), F32), pltpu.VMEM((64, 512), F32)],
        compiler_params=pltpu.CompilerParams(vmem_limit_bytes=16 * 2**20),
        name="choose",
    )(pairs, tile, far, own_fields, swapped, look)

    def to_core(value):
        return moved(value, lambda z, h, l, r: (z, h, l, r ^ 1))

    def to_chip(value):
        return moved(value, lambda z, h, l, r: (z, h, l, ((r + 1) ^ 1) - 1))

    beside = moved(fields, lambda z, h, l, r: (z, h, 1 - l, r))
    fields = jnp.concatenate([fields, beside], axis=0)
    core_fields = to_core(fields)
    chip_fields = to_chip(fields)
    filtered, coherence = pl.pallas_call(
        finish_kernel,
        out_shape=(jax.ShapeDtypeStruct((3, 2, 16, 32), F32), jax.ShapeDtypeStruct((3, 16, 32), F32)),
        in_specs=[VMEM] * 11,
        out_specs=(VMEM, VMEM),
        compiler_params=pltpu.CompilerParams(vmem_limit_bytes=24 * 2**20),
        name="finish",
    )(
        pairs,
        fields,
        core_fields,
        chip_fields,
        *[jnp.asarray(t) for t in tables()],
    )
    return (filtered[None], coherence[None])


def solution(mesh):
    placed = (P("tm", None, "az", "rg"), P("tm", None))
    return jax.shard_map(
        per_device,
        mesh=mesh,
        in_specs=placed,
        out_specs=(P("tm", None, None, "az", "rg"), P("tm", None, "az", "rg")),
        check_vma=False,
    )
```

```python
import math

import jax
import jax.numpy as jnp
import ml_dtypes
import numpy as np
from jax import lax
from jax.experimental import pallas as pl
from jax.experimental.pallas import tpu as pltpu
from jax.sharding import Mesh, PartitionSpec as P

F32 = jnp.float32
BF16 = jnp.bfloat16
EVERY = ("tm", "az", "rg")


def split_table(table):
    high = table.astype(ml_dtypes.bfloat16)
    low = (table - high.astype(np.float64)).astype(ml_dtypes.bfloat16)
    return high, low


def column_tables():
    forward = np.zeros((256, 384))
    back = np.zeros((256, 256))
    steps = np.arange(32)
    taper = np.sin(math.pi * (steps + 0.5) / 32.0) ** 2

    def row_of(field, column):
        if column < 16:
            return 128 + field * 32 + 16 + column
        if column < 48:
            return field * 32 + column - 16
        return 128 + field * 32 + column - 48

    for patch in range(3):
        for j in range(32):
            angle = 2.0 * math.pi * (j * steps % 32) / 32.0
            real, imag = row_of(0, patch * 16 + j), row_of(1, patch * 16 + j)
            at = patch * 32 + steps
            forward[real, at] = np.cos(angle)
            forward[imag, at] = np.sin(angle)
            forward[real, 128 + at] = -np.sin(angle)
            forward[imag, 128 + at] = np.cos(angle)
            column = patch * 16 + j - 16
            if 0 <= column < 32:
                scale = taper[j] / 32.0
                back[at, column] = np.cos(angle) * scale
                back[128 + at, column] = -np.sin(angle) * scale
                back[at, 128 + column] = np.sin(angle) * scale
                back[128 + at, 128 + column] = np.cos(angle) * scale
    for field in range(4):
        for cell in range(32):
            for column in range(cell + 14, cell + 19):
                forward[row_of(field, column), 256 + field * 32 + cell] = 1.0
    return forward, back


def line_tables():
    forward = np.zeros((2, 128, 64))
    window = np.zeros((2, 16, 32))
    back = np.zeros((32, 128))
    steps = np.arange(32)
    taper = np.sin(math.pi * (steps + 0.5) / 32.0) ** 2
    for side in range(2):
        places = {}
        for line in range(16):
            places[16 + line] = line
            places[(32 if side == 0 else 0) + line] = 16 + line
        for patch in range(2):
            for j in range(32):
                row = places.get(patch * 16 + j)
                if row is None:
                    continue
                angle = 2.0 * math.pi * (j * steps % 32) / 32.0
                at = patch * 32 + steps
                forward[side, at, row] = np.cos(angle)
                forward[side, at, 32 + row] = np.sin(angle)
                forward[side, 64 + at, row] = -np.sin(angle)
                forward[side, 64 + at, 32 + row] = np.cos(angle)
        for cell in range(16):
            for line in range(cell + 14, cell + 19):
                if line in places:
                    window[side, cell, places[line]] = 1.0
    for patch in range(2):
        for j in range(32):
            cell = patch * 16 + j - 16
            if 0 <= cell < 16:
                angle = 2.0 * math.pi * (j * steps % 32) / 32.0
                scale = taper[j] / 32.0
                at = patch * 32 + steps
                back[cell, at] = np.cos(angle) * scale
                back[cell, 64 + at] = -np.sin(angle) * scale
                back[16 + cell, at] = np.sin(angle) * scale
                back[16 + cell, 64 + at] = np.cos(angle) * scale
    return forward, window, back


def tables():
    column_forward, column_back = column_tables()
    line_forward, window, line_back = line_tables()
    cf_high, cf_low = split_table(column_forward)
    cb_high, cb_low = split_table(column_back)
    lf_high, lf_low = split_table(line_forward)
    lb_high, lb_low = split_table(line_back)
    return (
        cf_high,
        cf_low,
        np.concatenate([lf_high, lf_high, lf_low], axis=2),
        np.concatenate([window, window], axis=2).astype(ml_dtypes.bfloat16),
        np.concatenate([lb_high, lb_high, lb_low], axis=1),
        cb_high,
        cb_low,
    )


def look_table():
    table = np.zeros((512, 128))
    columns = np.arange(512)
    table[columns, columns // 16] = 1.0 / 64.0
    return table.astype(ml_dtypes.bfloat16)


def halves(values):
    high = values.astype(BF16)
    low = (values - high.astype(F32)).astype(BF16)
    return high, low


def dot(left, right):
    return jnp.dot(left, right, preferred_element_type=F32)


def widened(tiles, wide):
    for index, tile in enumerate(tiles):
        for part in range(2):
            for chunk in range(4):
                at = slice(chunk * 128, chunk * 128 + 128)
                wide[index * 2 + part, chunk] = tile[part, :, at].astype(F32)


def looked_fields(couples, powers, count, wide, sums, look):
    number = 2 * len(couples) + len(powers)
    for chunk in range(4):
        at = slice(chunk * 128, chunk * 128 + 128)
        totals = [None] * number
        for line in range(4):
            rows = pl.ds(line, 16, stride=4)
            real = [wide[2 * i, chunk, rows, :] for i in range(count)]
            imag = [wide[2 * i + 1, chunk, rows, :] for i in range(count)]
            terms = []
            for u, v in couples:
                terms.append(real[u] * real[v] + imag[u] * imag[v])
            for u, v in couples:
                terms.append(imag[u] * real[v] - real[u] * imag[v])
            for u in powers:
                terms.append(real[u] * real[u] + imag[u] * imag[u])
            totals = [t if s is None else s + t for s, t in zip(totals, terms)]
        for index, total in enumerate(totals):
            sums[index * 16 : index * 16 + 16, at] = total
    high, low = halves(sums[...])
    table = look[...]
    looked = dot(high, table) + dot(low, table)
    return [looked[i * 16 : i * 16 + 16] for i in range(number)]


def record(real, imag, far_power, own_power):
    crossed = real + pltpu.roll(imag, 32, 1)
    return crossed + pltpu.roll(far_power, 64, 1) + pltpu.roll(own_power, 96, 1)


def cross_kernel(own, other, up, down, look, own_out, other_out, powers, wide, sums):
    widened((own, other, up, down), wide)
    couples = ((0, 1), (0, 2), (0, 3), (1, 2), (1, 3))
    fields = looked_fields(couples, (0, 1, 2, 3), 4, wide, sums, look)
    power = fields[10:14]
    records = [record(fields[i], fields[5 + i], power[v], power[u]) for i, (u, v) in enumerate(couples)]
    for index in range(3):
        own_out[index] = records[index]
    for index in range(2):
        other_out[index] = records[3 + index]
    powers[...] = power[0]


def far_kernel(own, far, powers, look, out, wide, sums):
    widened((own, far), wide)
    fields = looked_fields(((0, 1),), (1,), 2, wide, sums, look)
    out[...] = record(fields[0], fields[1], fields[2], powers[...])


def offsets_of(pairs):
    position = lax.axis_index("tm")
    odd = position % 2 == 1
    offset = pairs[...] - position
    return odd, jnp.where(odd, -offset, offset)


def crossed_slots(flipped):
    return (flipped == 3) | (flipped == -1)


def choose_kernel(pairs, own, far, swapped, out):
    odd, flipped = offsets_of(pairs)
    up = jnp.where(odd, -2, 2)
    third = jnp.where(odd, swapped[1], swapped[0])
    first = jnp.where(odd, swapped[0], swapped[1])
    for slot in range(3):
        at = flipped[:, slot : slot + 1]
        chosen = jnp.where(at == 1, own[0], far[...])
        chosen = jnp.where(at == up, own[1], chosen)
        chosen = jnp.where(at == -up, own[2], chosen)
        chosen = jnp.where(at == 3, third, chosen)
        out[slot] = jnp.where(at == -1, first, chosen)


def finish_kernel(
    pairs,
    fields,
    chip_beside,
    chip,
    core_beside,
    beside,
    core,
    cf_high,
    cf_low,
    lf,
    window,
    lb,
    cb_high,
    cb_low,
    filtered,
    coherence,
):
    side = lax.axis_index("az")
    lane = lax.broadcasted_iota(jnp.int32, (1, 128), 1)
    place = lane % 32
    column = lax.axis_index("rg")
    from_core = (place >= 16) == (column % 2 == 1)
    inside = (column > 0) & (column < 7)

    def both(near, away):
        return jnp.concatenate([near[...].reshape(48, 128), away[...].reshape(48, 128)], axis=0)

    from_chip = jnp.where(inside, both(chip, chip_beside), 0.0)
    halo = jnp.where(from_core, both(core, core_beside), from_chip)
    values = jnp.concatenate([both(fields, beside), halo], axis=1)
    high, low = halves(values)
    table = cf_high[...]
    mixed = dot(high, table) + dot(low, table) + dot(high, cf_low[...])
    crossed = crossed_slots(offsets_of(pairs)[1])
    rows = []
    for slot in range(3):
        first, second = mixed[16 * slot : 16 * slot + 16], mixed[48 + 16 * slot : 64 + 16 * slot]
        turn = crossed[:, slot : slot + 1]
        rows.append(jnp.concatenate([jnp.where(turn, second, first), jnp.where(turn, first, second)], axis=0))
    real = jnp.concatenate([r[:, 0:128] for r in rows], axis=1)
    imag = jnp.concatenate([r[:, 128:256] for r in rows], axis=1)
    sums = jnp.concatenate([r[:, 256:384] for r in rows], axis=1)
    high, low = halves(jnp.concatenate([real, imag], axis=0))
    spectrum = dot(lf[side], jnp.concatenate([high, low, high], axis=0))
    spec_real, spec_imag = spectrum[0:64], spectrum[64:128]
    power = jnp.sqrt(spec_real * spec_real + spec_imag * spec_imag)

    def turned(block, by):
        away = pltpu.roll(block, by % 128, 1)
        wrapped = pltpu.roll(block, (by - 32) % 128, 1)
        if by > 0:
            return jnp.where(place < by, wrapped, away)
        wrapped = pltpu.roll(block, (by + 32) % 128, 1)
        return jnp.where(place >= 32 + by, wrapped, away)

    smoothed = []
    for patch in range(2):
        for slot in range(3):
            block = power[32 * patch : 32 * patch + 32, 128 * slot : 128 * slot + 128]
            block = block + pltpu.roll(block, 1, 0) + pltpu.roll(block, 31, 0)
            block = block + turned(block, 1) + turned(block, -1)
            smoothed.append(block / 9.0)
    largest = jnp.concatenate([jnp.max(b, axis=0, keepdims=True) for b in smoothed] + [jnp.zeros((2, 128), F32)], axis=0)
    groups = [jnp.max(jnp.where(lane // 32 == g, largest, 0.0), axis=1, keepdims=True) for g in range(3)]
    largest = jnp.where(lane < 32, groups[0], jnp.where(lane < 64, groups[1], groups[2]))
    scale = 1.0 / (jnp.sqrt(largest) + 1e-06)
    weights = [jnp.sqrt(b) * scale[i : i + 1] for i, b in enumerate(smoothed)]
    weights = jnp.concatenate(
        [jnp.concatenate(weights[0:3], axis=1), jnp.concatenate(weights[3:6], axis=1)], axis=0
    )
    high, low = halves(jnp.concatenate([spec_real * weights, spec_imag * weights], axis=0))
    lines = dot(lb[...], jnp.concatenate([high, low, high], axis=0))
    stacked = jnp.concatenate(
        [
            jnp.concatenate([lines[0:16, 128 * s : 128 * s + 128], lines[16:32, 128 * s : 128 * s + 128]], axis=1)
            for s in range(3)
        ],
        axis=0,
    )
    high, low = halves(stacked)
    table = cb_high[...]
    result = dot(high, table) + dot(low, table) + dot(high, cb_low[...])
    for slot in range(3):
        filtered[slot, 0] = result[16 * slot : 16 * slot + 16, 0:32]
        filtered[slot, 1] = result[16 * slot : 16 * slot + 16, 128:160]

    high, low = halves(sums)
    totals = dot(window[side], jnp.concatenate([high, low], axis=0))
    for slot in range(3):
        total = totals[:, 128 * slot : 128 * slot + 128]
        square = total * total
        square = square + pltpu.roll(square, 96, 1)
        product = total * pltpu.roll(total, 96, 1)
        product = pltpu.roll(product, 64, 1)
        coherence[slot] = (jnp.sqrt(square) / jnp.sqrt(product))[:, 0:32]


VMEM = pl.BlockSpec(memory_space=pltpu.VMEM)


def moved(value, where):
    pairs = []
    for z in range(8):
        for yh in range(2):
            for yl in range(2):
                for r in range(8):
                    tz, th, tl, tr = where(z, yh, yl, r)
                    if not 0 <= tz < 8:
                        tz, th, tl, tr = z, yh, yl, r ^ 1
                    if not 0 <= tr < 8:
                        tz, th, tl, tr = z, yh, 1 - yl, r
                    pairs.append((((z * 2 + yh) * 2 + yl) * 8 + r, ((tz * 2 + th) * 2 + tl) * 8 + tr))
    return lax.ppermute(value, EVERY, pairs)


def per_device(slc, pairs):
    tile = slc[0]
    position = lax.axis_index("tm")

    def even_pair(z, h, l, r):
        return (z ^ 1, h, l, r)

    def odd_pair(z, h, l, r):
        return (((z + 1) ^ 1) - 1, h, l, r)

    def far_pair(z, h, l, r):
        return (z - 2, 1, l, r) if h == 0 else (z + 2, 0, l, r)

    far = moved(tile, far_pair)
    swap_even = moved(tile, even_pair)
    swap_odd = moved(tile, odd_pair)
    other = moved(tile, lambda z, h, l, r: (z, 1 - h, l, r))
    even_z = (position // 2) % 2 == 0
    up = jnp.where(even_z, swap_even, swap_odd)
    down = jnp.where(even_z, swap_odd, swap_even)
    look = jnp.asarray(look_table())

    def looked(kernel, name, shapes, tiles, fields, operands):
        return pl.pallas_call(
            kernel,
            out_shape=[jax.ShapeDtypeStruct(shape, F32) for shape in shapes],
            in_specs=[VMEM] * len(operands),
            out_specs=[VMEM] * len(shapes),
            scratch_shapes=[pltpu.VMEM((2 * tiles, 4, 64, 128), F32), pltpu.VMEM((16 * fields, 512), F32)],
            compiler_params=pltpu.CompilerParams(vmem_limit_bytes=16 * 2**20),
            name=name,
        )(*operands)

    own_fields, other_fields, powers = looked(
        cross_kernel, "cross", ((3, 16, 128), (2, 16, 128), (16, 128)), 4, 14, (tile, other, up, down, look)
    )
    swapped = moved(other_fields, lambda z, h, l, r: (z, 1 - h, 1 - l, r))
    (away,) = looked(far_kernel, "far", ((16, 128),), 2, 3, (tile, far, powers, look))
    fields = pl.pallas_call(
        choose_kernel,
        out_shape=jax.ShapeDtypeStruct((3, 16, 128), F32),
        in_specs=[VMEM] * 4,
        out_specs=VMEM,
        compiler_params=pltpu.CompilerParams(vmem_limit_bytes=4 * 2**20),
        name="choose",
    )(pairs, own_fields, away, swapped)

    def chip_of(r):
        return ((r + 1) ^ 1) - 1

    halos = dict(
        beside=moved(fields, lambda z, h, l, r: (z, h, 1 - l, r)),
        core=moved(fields, lambda z, h, l, r: (z, h, l, r ^ 1)),
        chip=moved(fields, lambda z, h, l, r: (z, h, l, chip_of(r))),
        core_beside=moved(fields, lambda z, h, l, r: (z, h, 1 - l, r ^ 1)),
        chip_beside=moved(fields, lambda z, h, l, r: (z, h, 1 - l, chip_of(r))),
    )
    filtered, coherence = pl.pallas_call(
        finish_kernel,
        out_shape=(jax.ShapeDtypeStruct((3, 2, 16, 32), F32), jax.ShapeDtypeStruct((3, 16, 32), F32)),
        in_specs=[VMEM] * 14,
        out_specs=(VMEM, VMEM),
        compiler_params=pltpu.CompilerParams(vmem_limit_bytes=24 * 2**20),
        name="finish",
    )(
        pairs,
        fields,
        halos["chip_beside"],
        halos["chip"],
        halos["core_beside"],
        halos["beside"],
        halos["core"],
        *[jnp.asarray(t) for t in tables()],
    )
    return (filtered[None], coherence[None])


def solution(mesh):
    placed = (P("tm", None, "az", "rg"), P("tm", None))
    return jax.shard_map(
        per_device,
        mesh=mesh,
        in_specs=placed,
        out_specs=(P("tm", None, None, "az", "rg"), P("tm", None, "az", "rg")),
        check_vma=False,
    )
```

```python
import math

import jax
import jax.numpy as jnp
import ml_dtypes
import numpy as np
from jax import lax
from jax.experimental import pallas as pl
from jax.experimental.pallas import tpu as pltpu
from jax.sharding import Mesh, PartitionSpec as P

F32 = jnp.float32
BF16 = jnp.bfloat16
EVERY = ("tm", "az", "rg")


def split_table(table):
    high = table.astype(ml_dtypes.bfloat16)
    low = (table - high.astype(np.float64)).astype(ml_dtypes.bfloat16)
    return high, low


def column_tables():
    forward = np.zeros((256, 384))
    back = np.zeros((256, 256))
    steps = np.arange(32)
    taper = np.sin(math.pi * (steps + 0.5) / 32.0) ** 2

    def row_of(field, column):
        if column < 16:
            return 128 + field * 32 + 16 + column
        if column < 48:
            return field * 32 + column - 16
        return 128 + field * 32 + column - 48

    for patch in range(3):
        for j in range(32):
            angle = 2.0 * math.pi * (j * steps % 32) / 32.0
            real, imag = row_of(0, patch * 16 + j), row_of(1, patch * 16 + j)
            at = patch * 32 + steps
            forward[real, at] = np.cos(angle)
            forward[imag, at] = np.sin(angle)
            forward[real, 128 + at] = -np.sin(angle)
            forward[imag, 128 + at] = np.cos(angle)
            column = patch * 16 + j - 16
            if 0 <= column < 32:
                scale = taper[j] / 32.0
                back[at, column] = np.cos(angle) * scale
                back[128 + at, column] = -np.sin(angle) * scale
                back[at, 128 + column] = np.sin(angle) * scale
                back[128 + at, 128 + column] = np.cos(angle) * scale
    for field in range(4):
        for cell in range(32):
            for column in range(cell + 14, cell + 19):
                forward[row_of(field, column), 256 + field * 32 + cell] = 1.0
    return forward, back


def line_tables():
    forward = np.zeros((2, 128, 64))
    window = np.zeros((2, 16, 32))
    back = np.zeros((32, 128))
    steps = np.arange(32)
    taper = np.sin(math.pi * (steps + 0.5) / 32.0) ** 2
    for side in range(2):
        places = {}
        for line in range(16):
            places[16 + line] = line
            places[(32 if side == 0 else 0) + line] = 16 + line
        for patch in range(2):
            for j in range(32):
                row = places.get(patch * 16 + j)
                if row is None:
                    continue
                angle = 2.0 * math.pi * (j * steps % 32) / 32.0
                at = patch * 32 + steps
                forward[side, at, row] = np.cos(angle)
                forward[side, at, 32 + row] = np.sin(angle)
                forward[side, 64 + at, row] = -np.sin(angle)
                forward[side, 64 + at, 32 + row] = np.cos(angle)
        for cell in range(16):
            for line in range(cell + 14, cell + 19):
                if line in places:
                    window[side, cell, places[line]] = 1.0
    for patch in range(2):
        for j in range(32):
            cell = patch * 16 + j - 16
            if 0 <= cell < 16:
                angle = 2.0 * math.pi * (j * steps % 32) / 32.0
                scale = taper[j] / 32.0
                at = patch * 32 + steps
                back[cell, at] = np.cos(angle) * scale
                back[cell, 64 + at] = -np.sin(angle) * scale
                back[16 + cell, at] = np.sin(angle) * scale
                back[16 + cell, 64 + at] = np.cos(angle) * scale
    return forward, window, back


def tables():
    column_forward, column_back = column_tables()
    line_forward, window, line_back = line_tables()
    cf_high, cf_low = split_table(column_forward)
    cb_high, cb_low = split_table(column_back)
    lf_high, lf_low = split_table(line_forward)
    lb_high, lb_low = split_table(line_back)
    return (
        cf_high,
        cf_low,
        np.concatenate([lf_high, lf_high, lf_low], axis=2),
        np.concatenate([window, window], axis=2).astype(ml_dtypes.bfloat16),
        np.concatenate([lb_high, lb_high, lb_low], axis=1),
        cb_high,
        cb_low,
    )


def look_table():
    table = np.zeros((512, 128))
    columns = np.arange(512)
    table[columns, columns // 16] = 1.0 / 64.0
    return table.astype(ml_dtypes.bfloat16)


def halves(values):
    high = values.astype(BF16)
    low = (values - high.astype(F32)).astype(BF16)
    return high, low


def dot(left, right):
    return jnp.dot(left, right, preferred_element_type=F32)


def widened(tiles, wide):
    for index, tile in enumerate(tiles):
        for part in range(2):
            for chunk in range(4):
                at = slice(chunk * 128, chunk * 128 + 128)
                wide[index * 2 + part, chunk] = tile[part, :, at].astype(F32)


def looked_fields(couples, powers, count, wide, sums, look):
    number = 2 * len(couples) + len(powers)
    for chunk in range(4):
        at = slice(chunk * 128, chunk * 128 + 128)
        totals = [None] * number
        for line in range(4):
            rows = pl.ds(line, 16, stride=4)
            real = [wide[2 * i, chunk, rows, :] for i in range(count)]
            imag = [wide[2 * i + 1, chunk, rows, :] for i in range(count)]
            terms = []
            for u, v in couples:
                terms.append(real[u] * real[v] + imag[u] * imag[v])
            for u, v in couples:
                terms.append(imag[u] * real[v] - real[u] * imag[v])
            for u in powers:
                terms.append(real[u] * real[u] + imag[u] * imag[u])
            totals = [t if s is None else s + t for s, t in zip(totals, terms)]
        for index, total in enumerate(totals):
            sums[index * 16 : index * 16 + 16, at] = total
    high, low = halves(sums[...])
    table = look[...]
    looked = dot(high, table) + dot(low, table)
    return [looked[i * 16 : i * 16 + 16] for i in range(number)]


def record(real, imag, far_power, own_power):
    crossed = real + pltpu.roll(imag, 32, 1)
    return crossed + pltpu.roll(far_power, 64, 1) + pltpu.roll(own_power, 96, 1)


def cross_kernel(own, up, down, other, look, own_out, other_out, powers, wide, sums):
    widened((own, other, up, down), wide)
    couples = ((0, 1), (0, 2), (0, 3), (1, 2), (1, 3))
    fields = looked_fields(couples, (0, 1, 2, 3), 4, wide, sums, look)
    power = fields[10:14]
    records = [record(fields[i], fields[5 + i], power[v], power[u]) for i, (u, v) in enumerate(couples)]
    for index in range(3):
        own_out[index] = records[index]
    for index in range(2):
        other_out[index] = records[3 + index]
    powers[...] = power[0]


def far_kernel(own, far, powers, look, out, wide, sums):
    widened((own, far), wide)
    fields = looked_fields(((0, 1),), (1,), 2, wide, sums, look)
    out[...] = record(fields[0], fields[1], fields[2], powers[...])


def offsets_of(pairs):
    position = lax.axis_index("tm")
    odd = position % 2 == 1
    offset = pairs[...] - position
    return odd, jnp.where(odd, -offset, offset)


def crossed_slots(flipped):
    return (flipped == 3) | (flipped == -1)


def choose_kernel(pairs, own, far, swapped, out):
    odd, flipped = offsets_of(pairs)
    up = jnp.where(odd, -2, 2)
    third = jnp.where(odd, swapped[1], swapped[0])
    first = jnp.where(odd, swapped[0], swapped[1])
    for slot in range(3):
        at = flipped[:, slot : slot + 1]
        chosen = jnp.where(at == 1, own[0], far[...])
        chosen = jnp.where(at == up, own[1], chosen)
        chosen = jnp.where(at == -up, own[2], chosen)
        chosen = jnp.where(at == 3, third, chosen)
        out[slot] = jnp.where(at == -1, first, chosen)


def finish_kernel(
    pairs,
    fields,
    chip,
    chip_beside,
    core_beside,
    beside,
    core,
    cf_high,
    cf_low,
    lf,
    window,
    lb,
    cb_high,
    cb_low,
    filtered,
    coherence,
):
    side = lax.axis_index("az")
    lane = lax.broadcasted_iota(jnp.int32, (1, 128), 1)
    place = lane % 32
    column = lax.axis_index("rg")
    from_core = (place >= 16) == (column % 2 == 1)
    inside = (column > 0) & (column < 7)

    def both(near, away):
        return jnp.concatenate([near[...].reshape(48, 128), away[...].reshape(48, 128)], axis=0)

    from_chip = jnp.where(inside, both(chip, chip_beside), 0.0)
    halo = jnp.where(from_core, both(core, core_beside), from_chip)
    values = jnp.concatenate([both(fields, beside), halo], axis=1)
    high, low = halves(values)
    table = cf_high[...]
    mixed = dot(high, table) + dot(low, table)
    spread = mixed[:, 0:256] + dot(high, cf_low[:, 0:256])
    crossed = crossed_slots(offsets_of(pairs)[1])

    def by_slot(values):
        rows = []
        for slot in range(3):
            first, second = values[16 * slot : 16 * slot + 16], values[48 + 16 * slot : 64 + 16 * slot]
            turn = crossed[:, slot : slot + 1]
            rows.append(jnp.concatenate([jnp.where(turn, second, first), jnp.where(turn, first, second)], axis=0))
        return jnp.concatenate(rows, axis=1)

    real, imag, sums = by_slot(spread[:, 0:128]), by_slot(spread[:, 128:256]), by_slot(mixed[:, 256:384])
    high, low = halves(jnp.concatenate([real, imag], axis=0))
    spectrum = dot(lf[side], jnp.concatenate([high, low, high], axis=0))
    spec_real, spec_imag = spectrum[0:64], spectrum[64:128]
    power = jnp.sqrt(spec_real * spec_real + spec_imag * spec_imag)

    def turned(block, by):
        away = pltpu.roll(block, by % 128, 1)
        wrapped = pltpu.roll(block, (by - 32) % 128, 1)
        if by > 0:
            return jnp.where(place < by, wrapped, away)
        wrapped = pltpu.roll(block, (by + 32) % 128, 1)
        return jnp.where(place >= 32 + by, wrapped, away)

    smoothed = []
    for patch in range(2):
        for slot in range(3):
            block = power[32 * patch : 32 * patch + 32, 128 * slot : 128 * slot + 128]
            block = block + pltpu.roll(block, 1, 0) + pltpu.roll(block, 31, 0)
            block = block + turned(block, 1) + turned(block, -1)
            smoothed.append(block)
    largest = jnp.concatenate([jnp.max(b, axis=0, keepdims=True) for b in smoothed] + [jnp.zeros((2, 128), F32)], axis=0)
    groups = [jnp.max(jnp.where(lane // 32 == g, largest, 0.0), axis=1, keepdims=True) for g in range(3)]
    largest = jnp.where(lane < 32, groups[0], jnp.where(lane < 64, groups[1], groups[2]))
    scale = 1.0 / (jnp.sqrt(largest) + 3e-06)
    weights = [jnp.sqrt(b) * scale[i : i + 1] for i, b in enumerate(smoothed)]
    weights = jnp.concatenate(
        [jnp.concatenate(weights[0:3], axis=1), jnp.concatenate(weights[3:6], axis=1)], axis=0
    )
    high, low = halves(jnp.concatenate([spec_real * weights, spec_imag * weights], axis=0))
    lines = dot(lb[...], jnp.concatenate([high, low, high], axis=0))
    stacked = jnp.concatenate(
        [
            jnp.concatenate([lines[0:16, 128 * s : 128 * s + 128], lines[16:32, 128 * s : 128 * s + 128]], axis=1)
            for s in range(3)
        ],
        axis=0,
    )
    high, low = halves(stacked)
    table = cb_high[...]
    result = dot(high, table) + dot(low, table) + dot(high, cb_low[...])
    for slot in range(3):
        filtered[slot, 0] = result[16 * slot : 16 * slot + 16, 0:32]
        filtered[slot, 1] = result[16 * slot : 16 * slot + 16, 128:160]

    high, low = halves(sums)
    totals = dot(window[side], jnp.concatenate([high, low], axis=0))
    for slot in range(3):
        total = totals[:, 128 * slot : 128 * slot + 128]
        square = total * total
        square = square + pltpu.roll(square, 96, 1)
        product = total * pltpu.roll(total, 96, 1)
        product = pltpu.roll(product, 64, 1)
        coherence[slot] = (jnp.sqrt(square) / jnp.sqrt(product))[:, 0:32]


VMEM = pl.BlockSpec(memory_space=pltpu.VMEM)


def moved(value, where):
    pairs = []
    for z in range(8):
        for yh in range(2):
            for yl in range(2):
                for r in range(8):
                    tz, th, tl, tr = where(z, yh, yl, r)
                    if not 0 <= tz < 8:
                        tz, th, tl, tr = z, yh, yl, r ^ 1
                    if not 0 <= tr < 8:
                        tz, th, tl, tr = z, yh, 1 - yl, r
                    pairs.append((((z * 2 + yh) * 2 + yl) * 8 + r, ((tz * 2 + th) * 2 + tl) * 8 + tr))
    return lax.ppermute(value, EVERY, pairs)


def per_device(slc, pairs):
    tile = slc[0]
    position = lax.axis_index("tm")

    def even_pair(z, h, l, r):
        return (z ^ 1, h, l, r)

    def odd_pair(z, h, l, r):
        return (((z + 1) ^ 1) - 1, h, l, r)

    def far_pair(z, h, l, r):
        return (z - 2, 1, l, r) if h == 0 else (z + 2, 0, l, r)

    far = moved(tile, far_pair)
    swap_even = moved(tile, even_pair)
    swap_odd = moved(tile, odd_pair)
    other = moved(tile, lambda z, h, l, r: (z, 1 - h, l, r))
    even_z = (position // 2) % 2 == 0
    up = jnp.where(even_z, swap_even, swap_odd)
    down = jnp.where(even_z, swap_odd, swap_even)
    look = jnp.asarray(look_table())

    def looked(kernel, name, shapes, tiles, fields, operands):
        return pl.pallas_call(
            kernel,
            out_shape=[jax.ShapeDtypeStruct(shape, F32) for shape in shapes],
            in_specs=[VMEM] * len(operands),
            out_specs=[VMEM] * len(shapes),
            scratch_shapes=[pltpu.VMEM((2 * tiles, 4, 64, 128), F32), pltpu.VMEM((16 * fields, 512), F32)],
            compiler_params=pltpu.CompilerParams(vmem_limit_bytes=16 * 2**20),
            name=name,
        )(*operands)

    own_fields, other_fields, powers = looked(
        cross_kernel, "cross", ((3, 16, 128), (2, 16, 128), (16, 128)), 4, 14, (tile, up, down, other, look)
    )
    swapped = moved(other_fields, lambda z, h, l, r: (z, 1 - h, 1 - l, r))
    (away,) = looked(far_kernel, "far", ((16, 128),), 2, 3, (tile, far, powers, look))
    fields = pl.pallas_call(
        choose_kernel,
        out_shape=jax.ShapeDtypeStruct((3, 16, 128), F32),
        in_specs=[VMEM] * 4,
        out_specs=VMEM,
        compiler_params=pltpu.CompilerParams(vmem_limit_bytes=4 * 2**20),
        name="choose",
    )(pairs, own_fields, away, swapped)

    def chip_of(r):
        return ((r + 1) ^ 1) - 1

    halos = dict(
        beside=moved(fields, lambda z, h, l, r: (z, h, 1 - l, r)),
        core=moved(fields, lambda z, h, l, r: (z, h, l, r ^ 1)),
        chip=moved(fields, lambda z, h, l, r: (z, h, l, chip_of(r))),
        core_beside=moved(fields, lambda z, h, l, r: (z, h, 1 - l, r ^ 1)),
        chip_beside=moved(fields, lambda z, h, l, r: (z, h, 1 - l, chip_of(r))),
    )
    filtered, coherence = pl.pallas_call(
        finish_kernel,
        out_shape=(jax.ShapeDtypeStruct((3, 2, 16, 32), F32), jax.ShapeDtypeStruct((3, 16, 32), F32)),
        in_specs=[VMEM] * 14,
        out_specs=(VMEM, VMEM),
        compiler_params=pltpu.CompilerParams(vmem_limit_bytes=24 * 2**20),
        name="finish",
    )(
        pairs,
        fields,
        halos["chip"],
        halos["chip_beside"],
        halos["core_beside"],
        halos["beside"],
        halos["core"],
        *[jnp.asarray(t) for t in tables()],
    )
    return (filtered[None], coherence[None])


def solution(mesh):
    placed = (P("tm", None, "az", "rg"), P("tm", None))
    return jax.shard_map(
        per_device,
        mesh=mesh,
        in_specs=placed,
        out_specs=(P("tm", None, None, "az", "rg"), P("tm", None, "az", "rg")),
        check_vma=False,
    )
```

```python
import math

import jax
import jax.numpy as jnp
import ml_dtypes
import numpy as np
from jax import lax
from jax.experimental import pallas as pl
from jax.experimental.pallas import tpu as pltpu
from jax.sharding import Mesh, PartitionSpec as P

F32 = jnp.float32
BF16 = jnp.bfloat16
EVERY = ("tm", "az", "rg")


def split_table(table):
    high = table.astype(ml_dtypes.bfloat16)
    low = (table - high.astype(np.float64)).astype(ml_dtypes.bfloat16)
    return high, low


def column_tables():
    forward = np.zeros((256, 384))
    back = np.zeros((256, 256))
    steps = np.arange(32)
    taper = np.sin(math.pi * (steps + 0.5) / 32.0) ** 2

    def row_of(field, column):
        if column < 16:
            return 128 + field * 32 + 16 + column
        if column < 48:
            return field * 32 + column - 16
        return 128 + field * 32 + column - 48

    for patch in range(3):
        for j in range(32):
            angle = 2.0 * math.pi * (j * steps % 32) / 32.0
            real, imag = row_of(0, patch * 16 + j), row_of(1, patch * 16 + j)
            at = patch * 32 + steps
            forward[real, at] = np.cos(angle)
            forward[imag, at] = np.sin(angle)
            forward[real, 128 + at] = -np.sin(angle)
            forward[imag, 128 + at] = np.cos(angle)
            column = patch * 16 + j - 16
            if 0 <= column < 32:
                scale = taper[j] / 32.0
                back[at, column] = np.cos(angle) * scale
                back[128 + at, column] = -np.sin(angle) * scale
                back[at, 128 + column] = np.sin(angle) * scale
                back[128 + at, 128 + column] = np.cos(angle) * scale
    for field in range(4):
        for cell in range(32):
            for column in range(cell + 14, cell + 19):
                forward[row_of(field, column), 256 + field * 32 + cell] = 1.0
    return forward, back


def line_tables():
    forward = np.zeros((2, 128, 64))
    window = np.zeros((2, 16, 32))
    back = np.zeros((32, 128))
    steps = np.arange(32)
    taper = np.sin(math.pi * (steps + 0.5) / 32.0) ** 2
    for side in range(2):
        places = {}
        for line in range(16):
            places[16 + line] = line
            places[(32 if side == 0 else 0) + line] = 16 + line
        for patch in range(2):
            for j in range(32):
                row = places.get(patch * 16 + j)
                if row is None:
                    continue
                angle = 2.0 * math.pi * (j * steps % 32) / 32.0
                at = patch * 32 + steps
                forward[side, at, row] = np.cos(angle)
                forward[side, at, 32 + row] = np.sin(angle)
                forward[side, 64 + at, row] = -np.sin(angle)
                forward[side, 64 + at, 32 + row] = np.cos(angle)
        for cell in range(16):
            for line in range(cell + 14, cell + 19):
                if line in places:
                    window[side, cell, places[line]] = 1.0
    for patch in range(2):
        for j in range(32):
            cell = patch * 16 + j - 16
            if 0 <= cell < 16:
                angle = 2.0 * math.pi * (j * steps % 32) / 32.0
                scale = taper[j] / 32.0
                at = patch * 32 + steps
                back[cell, at] = np.cos(angle) * scale
                back[cell, 64 + at] = -np.sin(angle) * scale
                back[16 + cell, at] = np.sin(angle) * scale
                back[16 + cell, 64 + at] = np.cos(angle) * scale
    return forward, window, back


def tables():
    column_forward, column_back = column_tables()
    line_forward, window, line_back = line_tables()
    cf_high, cf_low = split_table(column_forward)
    cb_high, cb_low = split_table(column_back)
    lf_high, lf_low = split_table(line_forward)
    lb_high, lb_low = split_table(line_back)
    return (
        cf_high,
        cf_low,
        np.concatenate([lf_high, lf_high, lf_low], axis=2),
        np.concatenate([window, window], axis=2).astype(ml_dtypes.bfloat16),
        np.concatenate([lb_high, lb_high, lb_low], axis=1),
        cb_high,
        cb_low,
    )


def look_table():
    table = np.zeros((512, 128))
    columns = np.arange(512)
    table[columns, columns // 16] = 1.0 / 64.0
    return table.astype(ml_dtypes.bfloat16)


def halves(values):
    high = values.astype(BF16)
    low = (values - high.astype(F32)).astype(BF16)
    return high, low


def dot(left, right):
    return jnp.dot(left, right, preferred_element_type=F32)


def widened(tiles, wide):
    for index, tile in enumerate(tiles):
        for part in range(2):
            for chunk in range(4):
                at = slice(chunk * 128, chunk * 128 + 128)
                wide[index * 2 + part, chunk] = tile[part, :, at].astype(F32)


def looked_fields(couples, powers, count, wide, sums, look):
    number = 2 * len(couples) + len(powers)
    for chunk in range(4):
        at = slice(chunk * 128, chunk * 128 + 128)
        totals = [None] * number
        for line in range(4):
            rows = pl.ds(line, 16, stride=4)
            real = [wide[2 * i, chunk, rows, :] for i in range(count)]
            imag = [wide[2 * i + 1, chunk, rows, :] for i in range(count)]
            terms = []
            for u, v in couples:
                terms.append(real[u] * real[v] + imag[u] * imag[v])
            for u, v in couples:
                terms.append(imag[u] * real[v] - real[u] * imag[v])
            for u in powers:
                terms.append(real[u] * real[u] + imag[u] * imag[u])
            totals = [t if s is None else s + t for s, t in zip(totals, terms)]
        for index, total in enumerate(totals):
            sums[index * 16 : index * 16 + 16, at] = total
    high, low = halves(sums[...])
    table = look[...]
    looked = dot(high, table) + dot(low, table)
    return [looked[i * 16 : i * 16 + 16] for i in range(number)]


def record(real, imag, far_power, own_power):
    crossed = real + pltpu.roll(imag, 32, 1)
    return crossed + pltpu.roll(far_power, 64, 1) + pltpu.roll(own_power, 96, 1)


def line_kernel(own, up, down, look, out, powers, wide, sums):
    widened((own, up, down), wide)
    fields = looked_fields(((0, 1), (0, 2)), (0, 1, 2), 3, wide, sums, look)
    for index in range(2):
        out[index] = record(fields[index], fields[2 + index], fields[5 + index], fields[4])
    for index in range(3):
        powers[index] = fields[4 + index]


def cross_kernel(own, other, up, down, powers, look, near, other_out, power, wide, sums):
    widened((own, other, up, down), wide)
    fields = looked_fields(((0, 1), (1, 2), (1, 3)), (1,), 4, wide, sums, look)
    near[...] = record(fields[0], fields[3], fields[6], powers[0])
    for index in range(2):
        other_out[index] = record(fields[1 + index], fields[4 + index], powers[1 + index], fields[6])
    power[...] = powers[0]


def far_kernel(own, far, powers, look, out, wide, sums):
    widened((own, far), wide)
    fields = looked_fields(((0, 1),), (1,), 2, wide, sums, look)
    out[...] = record(fields[0], fields[1], fields[2], powers[...])


def offsets_of(pairs):
    position = lax.axis_index("tm")
    odd = position % 2 == 1
    offset = pairs[...] - position
    return odd, jnp.where(odd, -offset, offset)


def crossed_slots(flipped):
    return (flipped == 3) | (flipped == -1)


def choose_kernel(pairs, near, beyond, far, swapped, out):
    odd, flipped = offsets_of(pairs)
    up = jnp.where(odd, -2, 2)
    third = jnp.where(odd, swapped[1], swapped[0])
    first = jnp.where(odd, swapped[0], swapped[1])
    for slot in range(3):
        at = flipped[:, slot : slot + 1]
        chosen = jnp.where(at == 1, near[...], far[...])
        chosen = jnp.where(at == up, beyond[0], chosen)
        chosen = jnp.where(at == -up, beyond[1], chosen)
        chosen = jnp.where(at == 3, third, chosen)
        out[slot] = jnp.where(at == -1, first, chosen)


def finish_kernel(
    pairs,
    fields,
    chip_beside,
    chip,
    core_beside,
    beside,
    core,
    cf_high,
    cf_low,
    lf,
    window,
    lb,
    cb_high,
    cb_low,
    filtered,
    coherence,
):
    side = lax.axis_index("az")
    lane = lax.broadcasted_iota(jnp.int32, (1, 128), 1)
    place = lane % 32
    column = lax.axis_index("rg")
    from_core = (place >= 16) == (column % 2 == 1)
    inside = (column > 0) & (column < 7)

    def both(near, away):
        return jnp.concatenate([near[...].reshape(48, 128), away[...].reshape(48, 128)], axis=0)

    from_chip = jnp.where(inside, both(chip, chip_beside), 0.0)
    halo = jnp.where(from_core, both(core, core_beside), from_chip)
    values = jnp.concatenate([both(fields, beside), halo], axis=1)
    high, low = halves(values)
    table = cf_high[...]
    mixed = dot(high, table) + dot(low, table)
    spread = mixed[:, 0:256] + dot(high, cf_low[:, 0:256])
    crossed = crossed_slots(offsets_of(pairs)[1])

    def by_slot(values):
        rows = []
        for slot in range(3):
            first, second = values[16 * slot : 16 * slot + 16], values[48 + 16 * slot : 64 + 16 * slot]
            turn = crossed[:, slot : slot + 1]
            rows.append(jnp.concatenate([jnp.where(turn, second, first), jnp.where(turn, first, second)], axis=0))
        return jnp.concatenate(rows, axis=1)

    real, imag, sums = by_slot(spread[:, 0:128]), by_slot(spread[:, 128:256]), by_slot(mixed[:, 256:384])
    high, low = halves(jnp.concatenate([real, imag], axis=0))
    spectrum = dot(lf[side], jnp.concatenate([high, low, high], axis=0))
    spec_real, spec_imag = spectrum[0:64], spectrum[64:128]
    power = jnp.sqrt(spec_real * spec_real + spec_imag * spec_imag)

    def turned(block, by):
        away = pltpu.roll(block, by % 128, 1)
        wrapped = pltpu.roll(block, (by - 32) % 128, 1)
        if by > 0:
            return jnp.where(place < by, wrapped, away)
        wrapped = pltpu.roll(block, (by + 32) % 128, 1)
        return jnp.where(place >= 32 + by, wrapped, away)

    smoothed = []
    for patch in range(2):
        for slot in range(3):
            block = power[32 * patch : 32 * patch + 32, 128 * slot : 128 * slot + 128]
            block = block + pltpu.roll(block, 1, 0) + pltpu.roll(block, 31, 0)
            block = block + turned(block, 1) + turned(block, -1)
            smoothed.append(block)
    largest = jnp.concatenate([jnp.max(b, axis=0, keepdims=True) for b in smoothed] + [jnp.zeros((2, 128), F32)], axis=0)
    groups = [jnp.max(jnp.where(lane // 32 == g, largest, 0.0), axis=1, keepdims=True) for g in range(3)]
    largest = jnp.where(lane < 32, groups[0], jnp.where(lane < 64, groups[1], groups[2]))
    scale = 1.0 / (jnp.sqrt(largest) + 3e-06)
    weights = [jnp.sqrt(b) * scale[i : i + 1] for i, b in enumerate(smoothed)]
    weights = jnp.concatenate(
        [jnp.concatenate(weights[0:3], axis=1), jnp.concatenate(weights[3:6], axis=1)], axis=0
    )
    high, low = halves(jnp.concatenate([spec_real * weights, spec_imag * weights], axis=0))
    lines = dot(lb[...], jnp.concatenate([high, low, high], axis=0))
    stacked = jnp.concatenate(
        [
            jnp.concatenate([lines[0:16, 128 * s : 128 * s + 128], lines[16:32, 128 * s : 128 * s + 128]], axis=1)
            for s in range(3)
        ],
        axis=0,
    )
    high, low = halves(stacked)
    table = cb_high[...]
    result = dot(high, table) + dot(low, table) + dot(high, cb_low[...])
    for slot in range(3):
        filtered[slot, 0] = result[16 * slot : 16 * slot + 16, 0:32]
        filtered[slot, 1] = result[16 * slot : 16 * slot + 16, 128:160]

    high, low = halves(sums)
    totals = dot(window[side], jnp.concatenate([high, low], axis=0))
    for slot in range(3):
        total = totals[:, 128 * slot : 128 * slot + 128]
        square = total * total
        square = square + pltpu.roll(square, 96, 1)
        product = total * pltpu.roll(total, 96, 1)
        product = pltpu.roll(product, 64, 1)
        coherence[slot] = (jnp.sqrt(square) / jnp.sqrt(product))[:, 0:32]


VMEM = pl.BlockSpec(memory_space=pltpu.VMEM)


def moved(value, where):
    pairs = []
    for z in range(8):
        for yh in range(2):
            for yl in range(2):
                for r in range(8):
                    tz, th, tl, tr = where(z, yh, yl, r)
                    if not 0 <= tz < 8:
                        tz, th, tl, tr = z, yh, yl, r ^ 1
                    if not 0 <= tr < 8:
                        tz, th, tl, tr = z, yh, 1 - yl, r
                    pairs.append((((z * 2 + yh) * 2 + yl) * 8 + r, ((tz * 2 + th) * 2 + tl) * 8 + tr))
    return lax.ppermute(value, EVERY, pairs)


def per_device(slc, pairs):
    tile = slc[0]
    position = lax.axis_index("tm")

    def even_pair(z, h, l, r):
        return (z ^ 1, h, l, r)

    def odd_pair(z, h, l, r):
        return (((z + 1) ^ 1) - 1, h, l, r)

    def far_pair(z, h, l, r):
        return (z - 2, 1, l, r) if h == 0 else (z + 2, 0, l, r)

    far = moved(tile, far_pair)
    swap_even = moved(tile, even_pair)
    swap_odd = moved(tile, odd_pair)
    other = moved(tile, lambda z, h, l, r: (z, 1 - h, l, r))
    even_z = (position // 2) % 2 == 0
    up = jnp.where(even_z, swap_even, swap_odd)
    down = jnp.where(even_z, swap_odd, swap_even)
    look = jnp.asarray(look_table())

    def looked(kernel, name, shapes, tiles, fields, operands):
        return pl.pallas_call(
            kernel,
            out_shape=[jax.ShapeDtypeStruct(shape, F32) for shape in shapes],
            in_specs=[VMEM] * len(operands),
            out_specs=[VMEM] * len(shapes),
            scratch_shapes=[pltpu.VMEM((2 * tiles, 4, 64, 128), F32), pltpu.VMEM((16 * fields, 512), F32)],
            compiler_params=pltpu.CompilerParams(vmem_limit_bytes=16 * 2**20),
            name=name,
        )(*operands)

    beyond, line_powers = looked(line_kernel, "line", ((2, 16, 128), (3, 16, 128)), 3, 7, (tile, up, down, look))
    near, other_fields, powers = looked(
        cross_kernel,
        "cross",
        ((16, 128), (2, 16, 128), (16, 128)),
        4,
        7,
        (tile, other, up, down, line_powers, look),
    )
    swapped = moved(other_fields, lambda z, h, l, r: (z, 1 - h, 1 - l, r))
    (away,) = looked(far_kernel, "far", ((16, 128),), 2, 3, (tile, far, powers, look))
    fields = pl.pallas_call(
        choose_kernel,
        out_shape=jax.ShapeDtypeStruct((3, 16, 128), F32),
        in_specs=[VMEM] * 5,
        out_specs=VMEM,
        compiler_params=pltpu.CompilerParams(vmem_limit_bytes=4 * 2**20),
        name="choose",
    )(pairs, near, beyond, away, swapped)

    def chip_of(r):
        return ((r + 1) ^ 1) - 1

    halos = dict(
        beside=moved(fields, lambda z, h, l, r: (z, h, 1 - l, r)),
        core=moved(fields, lambda z, h, l, r: (z, h, l, r ^ 1)),
        chip=moved(fields, lambda z, h, l, r: (z, h, l, chip_of(r))),
        core_beside=moved(fields, lambda z, h, l, r: (z, h, 1 - l, r ^ 1)),
        chip_beside=moved(fields, lambda z, h, l, r: (z, h, 1 - l, chip_of(r))),
    )
    filtered, coherence = pl.pallas_call(
        finish_kernel,
        out_shape=(jax.ShapeDtypeStruct((3, 2, 16, 32), F32), jax.ShapeDtypeStruct((3, 16, 32), F32)),
        in_specs=[VMEM] * 14,
        out_specs=(VMEM, VMEM),
        compiler_params=pltpu.CompilerParams(vmem_limit_bytes=24 * 2**20),
        name="finish",
    )(
        pairs,
        fields,
        halos["chip_beside"],
        halos["chip"],
        halos["core_beside"],
        halos["beside"],
        halos["core"],
        *[jnp.asarray(t) for t in tables()],
    )
    return (filtered[None], coherence[None])


def solution(mesh):
    placed = (P("tm", None, "az", "rg"), P("tm", None))
    return jax.shard_map(
        per_device,
        mesh=mesh,
        in_specs=placed,
        out_specs=(P("tm", None, None, "az", "rg"), P("tm", None, "az", "rg")),
        check_vma=False,
    )
```
